32 devices in a mesh: grp: 2 (over y), pb: 8 (over z, x), layer: 2 (over core).
Axes of the slice: x: 2, y: 2, z: 4, core: 2. Of those that a mesh axis runs over, the one named last changes fastest.
Arguments:
- query_grads: bfloat16 [32768, 2, 1024], P(('grp', 'pb'), 'layer'), parts along dimension 0, may hold values from -0.19921875 to 0.19921875
- train_grads: bfloat16 [512, 2, 1024], P(('grp', 'pb'), 'layer'), parts along dimension 0, may hold values from -6 to 6
- basis_in: float32 [2, 32, 32], P('layer'), may hold values from -1 to 1, as said below
- basis_out: float32 [2, 32, 32], P('layer'), may hold values from -1 to 1, as said below
- eigenvalues: float32 [2, 32, 32], P('layer'), may hold values from 0.05 to 1
Outputs:
- scores: bfloat16 [32768, 256], P(('grp', 'pb', 'layer')), parts along dimension 0
The draws below stay inside these ranges and needn't reach their ends.
There are 2 independent parts, one for each index of `grp`. The reference program is written for one: setup_inputs(seed, part) draws one part's arguments, and reference() takes and returns one part's arrays. A program takes and returns all parts, laid end to end along the dimension named above; an argument that names none is the same for every part. Nothing has to cross between parts.
Inputs may be any that keep to these rules, and one draw needn't show every extreme that they name: `basis_in`: each layer's matrix is orthogonal. `basis_out`: each layer's matrix is orthogonal.
All inputs are finite; a program needn't handle non-finite values.
Results may differ from the reference program's by a relative error of at most 0.0076.
Values may be sent and summed in bfloat16 or wider, within the bound.
No kernel may reach another device: no remote copies, remote signals or barrier semaphores. Data moves between devices by JAX's collectives and lax.ppermute only.
A program may use at most 64 MiB of HBM per device.

```python
import math
import jax
import jax.numpy as jnp
from jax import lax

KOUT = 32
KIN = 32
GRAD = 1024
L_DEV = 1
LAYERS = 2
Q_DEV = 2048
QUERIES = 16384
TRAIN = 256


def orthogonal_basis(key, layers, dimension):
    order_key, column_key, flip_key = jax.random.split(key, 3)

    def shuffled(subkey):
        return jax.random.permutation(subkey, dimension)
    frequency = jax.vmap(shuffled)(jax.random.split(order_key, layers))
    position = jax.vmap(shuffled)(jax.random.split(column_key, layers))
    sign_flip = (2 * jax.random.randint(flip_key, (layers, dimension), 0, 2) - 1).astype(jnp.float32)
    frequency = frequency.astype(jnp.float32)[:, :, None]
    position = position.astype(jnp.float32)[:, None, :]
    row_scale = jnp.where(frequency == 0.0, math.sqrt(1.0 / dimension), math.sqrt(2.0 / dimension))
    angles = math.pi * (position + 0.5) * frequency / dimension
    return (sign_flip[:, :, None] * row_scale * jnp.cos(angles)).astype(jnp.float32)


def draw_basis_in(key, part):
    key = jax.random.fold_in(key, 11)
    return orthogonal_basis(key, LAYERS, KIN)


def draw_basis_out(key, part):
    key = jax.random.fold_in(key, 23)
    return orthogonal_basis(key, LAYERS, KOUT)


def level_of(own_key, extent, cuts, smallest, largest):
    gain, own = 1.0, jax.random.fold_in(own_key, 6)
    for axis_at, blocks in cuts:
        heights = jnp.exp(jax.random.uniform(jax.random.fold_in(own, axis_at), (blocks,), jnp.float32, smallest / len(cuts), largest / len(cuts)))
        gain = gain * jnp.repeat(heights, extent[axis_at] // blocks).reshape([-1 if axis == axis_at else 1 for axis in range(len(extent))])
    return gain


def noise(stream_key, extent, deviation, most, cuts=(), kind=jnp.bfloat16):
    entries = deviation * jax.random.normal(stream_key, extent, jnp.float32)
    if cuts:
        entries = entries * level_of(stream_key, extent, cuts, -0.22, 0.18)
    return jnp.clip(entries, -most, most).astype(kind)


def setup_inputs(seed: int = 0, part: int = 0) -> dict:
    seeds = jax.random.split(jax.random.key(seed), 6)
    own_keys = jax.random.split(jax.random.fold_in(seeds[5], part), 6)
    return {
        "query_grads": noise(own_keys[0], (QUERIES, LAYERS, GRAD), 0.03125, 0.19921875, ((0, 8), (1, 2))),
        "train_grads": noise(own_keys[1], (TRAIN, LAYERS, GRAD), 1.0, 6.0, ((0, 8), (1, 2))),
        "basis_in": draw_basis_in(jax.random.fold_in(seeds[5], 71), part),
        "basis_out": draw_basis_out(jax.random.fold_in(seeds[5], 71), part),
        "eigenvalues": jnp.clip(jnp.exp(math.log(1.0) - 2.9957323 * jax.random.uniform(seeds[4], (LAYERS, KOUT, KIN), jnp.float32) ** level_of(seeds[4], (LAYERS, KOUT, KIN), ((0, 2),), -0.2, 0.2)), 0.05, 1.0),
    }


def kron_bases(basis_in, basis_out):
    layers = basis_in.shape[0]
    whole = basis_out[:, :, None, :, None] * basis_in[:, None, :, None, :]
    return whole.reshape(layers, KOUT * KIN, KOUT * KIN).astype(jnp.bfloat16)


def precondition(grads, kron, eigenvalues):
    rows = grads.shape[0]
    layers = grads.shape[1]
    high = lax.Precision.HIGHEST
    kron_wide = kron.astype(jnp.float32)
    rotated = jnp.einsum("qlg,lgh->qlh", grads.astype(jnp.float32), kron_wide, precision=high)
    scaled = (rotated / (eigenvalues.reshape(layers, KOUT * KIN)[None] + 0.1)).astype(jnp.bfloat16)
    back = jnp.einsum("qlh,lgh->qlg", scaled.astype(jnp.float32), kron_wide, precision=high)
    return back.astype(jnp.bfloat16)


def reference(query_grads, train_grads, basis_in, basis_out, eigenvalues):
    groups = LAYERS // L_DEV
    kron = kron_bases(basis_in, basis_out)
    train_parts = [train_grads[:, g * L_DEV:(g + 1) * L_DEV].reshape(TRAIN, L_DEV * GRAD) for g in range(groups)]
    blocks = query_grads.reshape(QUERIES // Q_DEV, Q_DEV, LAYERS, GRAD)

    def score_block(block):
        prepared = precondition(block, kron, eigenvalues)
        total = jnp.zeros((Q_DEV, TRAIN), jnp.float32)
        for g in range(groups):
            left = prepared[:, g * L_DEV:(g + 1) * L_DEV].reshape(Q_DEV, L_DEV * GRAD)
            term = lax.dot_general(left, train_parts[g], (((1,), (1,)), ((), ())), preferred_element_type=jnp.float32)
            term = lax.optimization_barrier(term.astype(jnp.bfloat16))
            total = total + term.astype(jnp.float32)
        return total.astype(jnp.bfloat16)

    return lax.map(score_block, blocks).reshape(QUERIES, TRAIN)
```

```python
import functools

import jax
import jax.numpy as jnp
from jax import lax
from jax.experimental import pallas as pl
from jax.experimental.pallas import tpu as pltpu
from jax.sharding import PartitionSpec as P

F32, BF16 = jnp.float32, jnp.bfloat16
VMEM = pl.BlockSpec(memory_space=pltpu.VMEM)
HIGH = lax.Precision.HIGHEST
NT = (((1,), (1,)), ((), ()))
LIMIT = 24 * 1024 * 1024


def chunk(size, most):
    return most if size % most == 0 else size


def curvature_kernel(basis_in_ref, basis_out_ref, eigen_ref, m_ref, kron_ref, scaled_ref):
    kout, kin = basis_out_ref.shape[1], basis_in_ref.shape[1]
    grad = kout * kin
    lane_out = lax.broadcasted_iota(jnp.int32, (kout, grad), 1) // kin
    repeat = (lax.broadcasted_iota(jnp.int32, (kout, grad), 0) == lane_out).astype(F32)
    lane_in = lax.broadcasted_iota(jnp.int32, (kin, grad), 1) % kin
    tile = (lax.broadcasted_iota(jnp.int32, (kin, grad), 0) == lane_in).astype(F32)
    tiled_in = jnp.dot(basis_in_ref[0], tile, precision=HIGH, preferred_element_type=F32)
    spread_out = jnp.dot(basis_out_ref[0], repeat, precision=HIGH, preferred_element_type=F32)
    tiled_eigen = jnp.dot(eigen_ref[0], tile, precision=HIGH, preferred_element_type=F32)
    inverse = 1.0 / (jnp.sum(tiled_eigen * repeat, axis=0, keepdims=True) + 0.1)
    for b in range(kout):
        rows = (spread_out[b:b + 1, :] * tiled_in).astype(BF16)
        kron_ref[pl.ds(b * kin, kin), :] = rows
        scaled_ref[pl.ds(b * kin, kin), :] = (rows.astype(F32) * inverse).astype(BF16)
    step = chunk(grad, 256)

    @pl.loop(0, grad // step)
    def _(i):
        rows = pl.ds(pl.multiple_of(i * step, step), step)
        m_ref[rows, :] = lax.dot_general(scaled_ref[rows, :], kron_ref[...], NT, preferred_element_type=F32).astype(BF16)


def curvature(basis_in, basis_out, eigenvalues):
    grad = basis_in.shape[1] * basis_out.shape[1]
    return pl.pallas_call(
        curvature_kernel,
        out_shape=jax.ShapeDtypeStruct((grad, grad), BF16),
        in_specs=[VMEM] * 3,
        out_specs=VMEM,
        scratch_shapes=[pltpu.VMEM((grad, grad), BF16)] * 2,
        compiler_params=pltpu.CompilerParams(vmem_limit_bytes=LIMIT),
        cost_estimate=pl.CostEstimate(flops=2 * grad**3, bytes_accessed=2 * grad**2, transcendentals=0),
        name="curvature",
    )(basis_in, basis_out, eigenvalues)


def outgoing_kernel(masks, *refs):
    n = len(masks)
    blocks, (m_ref, q_ref, w_ref, out_ref, t_ref) = refs[:n], refs[n:]
    half = out_ref.shape[0]
    me = lax.axis_index("pb")
    for block, mask in zip(blocks, masks):
        size = block.shape[0]
        row = 0 if mask is None else pl.multiple_of((me ^ mask) * size, size)
        t_ref[pl.ds(row, size), :] = block[...]
    train = t_ref.shape[0]
    step = chunk(train, 256)
    other = 1 - lax.axis_index("layer")

    @pl.loop(0, train // step)
    def _(i):
        rows = pl.ds(pl.multiple_of(i * step, step), step)
        w_ref[rows, :] = jnp.dot(t_ref[rows, :], m_ref[...], preferred_element_type=F32).astype(BF16)

    qstep = chunk(half, 256)

    @pl.loop(0, half // qstep)
    def _(i):
        rows = pl.ds(pl.multiple_of(i * qstep, qstep), qstep)
        left = q_ref[pl.ds(pl.multiple_of(other * half + i * qstep, qstep), qstep), :]
        out_ref[rows, :] = lax.dot_general(left, w_ref[...], NT, preferred_element_type=F32).astype(BF16)


def outgoing(blocks, masks, m, q):
    train = sum(block.shape[0] for block in blocks)
    half, grad = q.shape[0] // 2, q.shape[1]
    return pl.pallas_call(
        functools.partial(outgoing_kernel, masks),
        out_shape=(jax.ShapeDtypeStruct((train, grad), BF16), jax.ShapeDtypeStruct((half, train), BF16)),
        in_specs=[VMEM] * (len(blocks) + 2),
        out_specs=(VMEM, VMEM),
        scratch_shapes=[pltpu.VMEM((train, grad), BF16)],
        compiler_params=pltpu.CompilerParams(vmem_limit_bytes=LIMIT),
        cost_estimate=pl.CostEstimate(flops=2 * train * grad * (grad + half), bytes_accessed=2 * half * grad, transcendentals=0),
        name="outgoing",
    )(*blocks, m, q)


def own_kernel(w_ref, q_ref, out_ref):
    half = out_ref.shape[0]
    own = lax.axis_index("layer")
    step = chunk(half, 256)

    @pl.loop(0, half // step)
    def _(i):
        rows = pl.ds(pl.multiple_of(i * step, step), step)
        left = q_ref[pl.ds(pl.multiple_of(own * half + i * step, step), step), :]
        out_ref[rows, :] = lax.dot_general(left, w_ref[...], NT, preferred_element_type=F32)


def own_scores(w, q):
    train, (half, grad) = w.shape[0], (q.shape[0] // 2, q.shape[1])
    return pl.pallas_call(
        own_kernel,
        out_shape=jax.ShapeDtypeStruct((half, train), F32),
        in_specs=[VMEM, VMEM],
        out_specs=VMEM,
        compiler_params=pltpu.CompilerParams(vmem_limit_bytes=LIMIT),
        cost_estimate=pl.CostEstimate(flops=2 * train * grad * half, bytes_accessed=2 * half * grad, transcendentals=0),
        name="own_scores",
    )(w, q)


def swap(x, n, mask):
    return lax.ppermute(x, "pb", [(i, i ^ mask) for i in range(n)])


def on_device(n, query_grads, train_grads, basis_in, basis_out, eigenvalues):
    train = train_grads.reshape(train_grads.shape[0], -1)
    queries = query_grads.reshape(query_grads.shape[0], -1)
    m = curvature(basis_in, basis_out, eigenvalues)
    if n == 8:
        far = [swap(train, n, mask) for mask in (4, 6)]
        near = [swap(train, n, mask) for mask in (2, 1, 3)]
        relayed = [swap(block, n, 1) for block in far]
        blocks, masks = [train] + far + near + relayed, (0, 4, 6, 2, 1, 3, 5, 7)
    else:
        blocks, masks = [lax.all_gather(train, "pb", axis=0, tiled=True)], (None,)
    w, sent = outgoing(blocks, masks, m, queries)
    received = lax.ppermute(sent, "layer", [(0, 1), (1, 0)])
    own = own_scores(w, queries)
    return (own + received.astype(F32)).astype(BF16)


def solution(mesh):
    placed = (
        P(("grp", "pb"), "layer", None),
        P(("grp", "pb"), "layer", None),
        P("layer", None, None),
        P("layer", None, None),
        P("layer", None, None),
    )
    return jax.shard_map(
        functools.partial(on_device, mesh.shape["pb"]),
        mesh=mesh,
        in_specs=placed,
        out_specs=P(("grp", "pb", "layer"), None),
        check_vma=False,
    )
```

```python
import functools

import jax
import jax.numpy as jnp
from jax import lax
from jax.experimental import pallas as pl
from jax.experimental.pallas import tpu as pltpu
from jax.sharding import PartitionSpec as P

F32, BF16 = jnp.float32, jnp.bfloat16
VMEM = pl.BlockSpec(memory_space=pltpu.VMEM)
HBM = pl.BlockSpec(memory_space=pl.ANY)
HIGH = lax.Precision.HIGHEST
NT = (((1,), (1,)), ((), ()))
PARAMS = pltpu.CompilerParams(vmem_limit_bytes=24 * 1024 * 1024)


def estimate(flops, bytes_accessed):
    return pl.CostEstimate(flops=flops, bytes_accessed=bytes_accessed, transcendentals=0)


def kron_kernel(in_hbm, out_hbm, eigen_hbm, kron_ref, inverse_ref, basis_in, basis_out, eigen, sems):
    pairs = ((in_hbm, basis_in), (out_hbm, basis_out), (eigen_hbm, eigen))
    copies = [pltpu.make_async_copy(*pair, sems.at[i]) for i, pair in enumerate(pairs)]
    for copy in copies:
        copy.start()
    kout, kin = basis_out.shape[1], basis_in.shape[1]
    grad = kout * kin
    lane_out = lax.broadcasted_iota(jnp.int32, (kout, grad), 1) // kin
    repeat = (lax.broadcasted_iota(jnp.int32, (kout, grad), 0) == lane_out).astype(F32)
    lane_in = lax.broadcasted_iota(jnp.int32, (kin, grad), 1) % kin
    tile = (lax.broadcasted_iota(jnp.int32, (kin, grad), 0) == lane_in).astype(F32)
    for copy in copies:
        copy.wait()
    tiled_in = jnp.dot(basis_in[0], tile, precision=HIGH, preferred_element_type=F32)
    spread_out = jnp.dot(basis_out[0], repeat, precision=HIGH, preferred_element_type=F32)
    tiled_eigen = jnp.dot(eigen[0], tile, precision=HIGH, preferred_element_type=F32)
    inverse_ref[...] = 1.0 / (jnp.sum(tiled_eigen * repeat, axis=0, keepdims=True) + 0.1)
    for b in range(kout):
        kron_ref[pl.ds(b * kin, kin), :] = (spread_out[b:b + 1, :] * tiled_in).astype(BF16)


def kron_bases(basis_in, basis_out, eigenvalues):
    grad = basis_in.shape[1] * basis_out.shape[1]
    return pl.pallas_call(
        kron_kernel,
        out_shape=tuple(jax.ShapeDtypeStruct(*x) for x in (((grad, grad), BF16), ((1, grad), F32))),
        in_specs=[HBM] * 3,
        out_specs=(VMEM,) * 2,
        scratch_shapes=[pltpu.VMEM(x.shape, F32) for x in (basis_in, basis_out, eigenvalues)] + [pltpu.SemaphoreType.DMA((3,))],
        compiler_params=PARAMS,
        cost_estimate=estimate(4 * grad**3, 0),
        name="kron_bases",
    )(*(pltpu.with_memory_space_constraint(x, pltpu.HBM) for x in (basis_in, basis_out, eigenvalues)))


def fill_rows(masks, blocks, kron_ref, inverse_ref, w_ref, rows_ref):
    size = blocks[0].shape[0]
    for i, block in enumerate(blocks):
        rows_ref[pl.ds(i * size, size), :] = block[...]
    total = len(blocks) * size
    step = min(total, 256)
    for i in range(total // step):
        rows = pl.ds(i * step, step)
        rotated = jnp.dot(rows_ref[rows, :], kron_ref[...], preferred_element_type=F32)
        scaled = (rotated * inverse_ref[...]).astype(BF16)
        rows_ref[rows, :] = lax.dot_general(scaled, kron_ref[...], NT, preferred_element_type=F32).astype(BF16)
    me = lax.axis_index("pb")
    for i, mask in enumerate(masks):
        at = pl.multiple_of((me ^ mask) * size, size) if len(masks) > 1 else 0
        w_ref[pl.ds(at, size), :] = rows_ref[pl.ds(i * size, size), :]


def score_half(layer, q_ref, w_ref, out_ref):
    half, step = out_ref.shape[0], min(w_ref.shape[0], 256)
    rows = pl.ds(pl.multiple_of(layer * half, half), half)
    for i in range(w_ref.shape[0] // step):
        cols = slice(i * step, (i + 1) * step)
        product = lax.dot_general(q_ref[rows, :], w_ref[cols, :], NT, preferred_element_type=F32)
        out_ref[:, cols] = product.astype(out_ref.dtype)


def early_kernel(masks, *refs):
    *blocks, kron_ref, inverse_ref, w_ref, rows_ref = refs
    fill_rows(masks, blocks, kron_ref, inverse_ref, w_ref, rows_ref)


def late_kernel(masks, *refs):
    *blocks, kron_ref, inverse_ref, _, q_ref, w_ref, out_ref, rows_ref = refs
    if blocks:
        fill_rows(masks, blocks, kron_ref, inverse_ref, w_ref, rows_ref)
    score_half(1 - lax.axis_index("layer"), q_ref, w_ref, out_ref)


def own_kernel(w_ref, q_ref, out_ref):
    score_half(lax.axis_index("layer"), q_ref, w_ref, out_ref)


def early_rows(masks, blocks, kron, inverse, train):
    rows, grad = sum(block.shape[0] for block in blocks), kron.shape[0]
    return pl.pallas_call(
        functools.partial(early_kernel, masks),
        out_shape=jax.ShapeDtypeStruct((train, grad), BF16),
        in_specs=[VMEM] * (len(blocks) + 2),
        out_specs=VMEM,
        scratch_shapes=[pltpu.VMEM((rows, grad), BF16)],
        compiler_params=PARAMS,
        cost_estimate=estimate(0, 0),
        name="early_rows",
    )(*blocks, kron, inverse)


def outgoing_scores(masks, blocks, kron, inverse, w, queries):
    rows, (train, grad), half = sum(block.shape[0] for block in blocks), w.shape, queries.shape[0] // 2
    return pl.pallas_call(
        functools.partial(late_kernel, masks),
        out_shape=(jax.ShapeDtypeStruct((train, grad), BF16), jax.ShapeDtypeStruct((half, train), BF16)),
        in_specs=[VMEM] * (len(blocks) + 4),
        out_specs=(VMEM, VMEM),
        input_output_aliases={len(blocks) + 2: 0},
        scratch_shapes=[pltpu.VMEM((max(rows, 32), grad), BF16)],
        compiler_params=PARAMS,
        cost_estimate=estimate(2 * train * grad * half, 2 * half * grad),
        name="outgoing_scores",
    )(*blocks, kron, inverse, w, queries)


def own_scores(w, queries):
    (train, grad), half = w.shape, queries.shape[0] // 2
    return pl.pallas_call(
        own_kernel,
        out_shape=jax.ShapeDtypeStruct((half, train), F32),
        in_specs=[VMEM, VMEM],
        out_specs=VMEM,
        compiler_params=PARAMS,
        cost_estimate=estimate(2 * train * grad * half, 2 * half * grad),
        name="own_scores",
    )(w, queries)


def exchange(x, n, mask):
    return lax.ppermute(x, "pb", [(i, i ^ mask) for i in range(n)])


def on_device(n, query_grads, train_grads, basis_in, basis_out, eigenvalues):
    train = train_grads.reshape(train_grads.shape[0], -1)
    queries = query_grads.reshape(query_grads.shape[0], -1)
    if n == 8:
        far = [exchange(train, n, mask) for mask in (4, 6)]
        near = [exchange(train, n, mask) for mask in (2, 1, 3)]
        early, late = [train] + far + near, [exchange(block, n, 1) for block in far]
        early_masks, late_masks = (0, 4, 6, 2, 1, 3), (5, 7)
        basis_in, basis_out, eigenvalues, _ = lax.optimization_barrier((basis_in, basis_out, eigenvalues, far[0]))
    else:
        early, late = [lax.all_gather(train, "pb", axis=0, tiled=True)], []
        early_masks, late_masks = (0,), ()
    kron, inverse = kron_bases(basis_in, basis_out, eigenvalues)
    w = early_rows(early_masks, early, kron, inverse, n * train.shape[0])
    w, sent = outgoing_scores(late_masks, late, kron, inverse, w, queries)
    received = lax.ppermute(sent, "layer", [(0, 1), (1, 0)])
    return (own_scores(w, queries) + received.astype(F32)).astype(BF16)


def solution(mesh):
    placed = (
        P(("grp", "pb"), "layer", None),
        P(("grp", "pb"), "layer", None),
        P("layer", None, None),
        P("layer", None, None),
        P("layer", None, None),
    )
    return jax.shard_map(
        functools.partial(on_device, mesh.shape["pb"]),
        mesh=mesh,
        in_specs=placed,
        out_specs=P(("grp", "pb", "layer"), None),
        check_vma=False,
    )
```

```python
import functools

import jax
import jax.numpy as jnp
from jax import lax
from jax.experimental import pallas as pl
from jax.experimental.pallas import tpu as pltpu
from jax.sharding import PartitionSpec as P

F32, BF16 = jnp.float32, jnp.bfloat16
VMEM = pl.BlockSpec(memory_space=pltpu.VMEM)
HBM = pl.BlockSpec(memory_space=pl.ANY)
HIGH = lax.Precision.HIGHEST
NT = (((1,), (1,)), ((), ()))
PARAMS = pltpu.CompilerParams(vmem_limit_bytes=24 * 1024 * 1024)


def estimate(flops, bytes_accessed):
    return pl.CostEstimate(flops=flops, bytes_accessed=bytes_accessed, transcendentals=0)


def kron_kernel(in_hbm, out_hbm, eigen_hbm, kron_ref, inverse_ref, basis_in, basis_out, eigen, sems):
    pairs = ((in_hbm, basis_in), (out_hbm, basis_out), (eigen_hbm, eigen))
    copies = [pltpu.make_async_copy(*pair, sems.at[i]) for i, pair in enumerate(pairs)]
    for copy in copies:
        copy.start()
    kout, kin = basis_out.shape[1], basis_in.shape[1]
    grad = kout * kin
    lane_out = lax.broadcasted_iota(jnp.int32, (kout, grad), 1) // kin
    repeat = (lax.broadcasted_iota(jnp.int32, (kout, grad), 0) == lane_out).astype(F32)
    lane_in = lax.broadcasted_iota(jnp.int32, (kin, grad), 1) % kin
    tile = (lax.broadcasted_iota(jnp.int32, (kin, grad), 0) == lane_in).astype(F32)
    for copy in copies:
        copy.wait()
    tiled_in = jnp.dot(basis_in[0], tile, precision=HIGH, preferred_element_type=F32)
    spread_out = jnp.dot(basis_out[0], repeat, precision=HIGH, preferred_element_type=F32)
    tiled_eigen = jnp.dot(eigen[0], tile, precision=HIGH, preferred_element_type=F32)
    inverse_ref[...] = 1.0 / (jnp.sum(tiled_eigen * repeat, axis=0, keepdims=True) + 0.1)
    for b in range(kout):
        kron_ref[pl.ds(b * kin, kin), :] = (spread_out[b:b + 1, :] * tiled_in).astype(BF16)


def kron_bases(basis_in, basis_out, eigenvalues):
    grad = basis_in.shape[1] * basis_out.shape[1]
    return pl.pallas_call(
        kron_kernel,
        out_shape=tuple(jax.ShapeDtypeStruct(*x) for x in (((grad, grad), BF16), ((1, grad), F32))),
        in_specs=[HBM] * 3,
        out_specs=(VMEM,) * 2,
        scratch_shapes=[pltpu.VMEM(x.shape, F32) for x in (basis_in, basis_out, eigenvalues)] + [pltpu.SemaphoreType.DMA((3,))],
        compiler_params=PARAMS,
        cost_estimate=estimate(4 * grad**3, 0),
        name="kron_bases",
    )(*(pltpu.with_memory_space_constraint(x, pltpu.HBM) for x in (basis_in, basis_out, eigenvalues)))


def precondition_kernel(*refs):
    *blocks, kron_ref, inverse_ref, w_ref = refs
    size, total = blocks[0].shape[0], w_ref.shape[0]
    for i, block in enumerate(blocks):
        w_ref[pl.ds(i * size, size), :] = block[...]
    step = min(total, 256)
    for i in range(total // step):
        rows = pl.ds(i * step, step)
        rotated = jnp.dot(w_ref[rows, :], kron_ref[...], preferred_element_type=F32)
        scaled = (rotated * inverse_ref[...]).astype(BF16)
        w_ref[rows, :] = lax.dot_general(scaled, kron_ref[...], NT, preferred_element_type=F32).astype(BF16)


def precondition(blocks, kron, inverse, name):
    rows, grad = sum(block.shape[0] for block in blocks), kron.shape[0]
    return pl.pallas_call(
        precondition_kernel,
        out_shape=jax.ShapeDtypeStruct((rows, grad), BF16),
        in_specs=[VMEM] * (len(blocks) + 2),
        out_specs=VMEM,
        compiler_params=PARAMS,
        cost_estimate=estimate(0, 0),
        name=name,
    )(*blocks, kron, inverse)


def arrange(masks, groups, w_ref):
    me, size = lax.axis_index("pb"), w_ref.shape[0] // len(masks)
    i = 0
    for group in groups:
        for row in range(0, group.shape[0], size):
            at = pl.multiple_of((me ^ masks[i]) * size, size) if len(masks) > 1 else 0
            w_ref[pl.ds(at, size), :] = group[pl.ds(row, size), :]
            i += 1


def first_kernel(masks, *refs):
    *groups, q_ref, out_ref, w_ref = refs
    arrange(masks, groups, w_ref)
    half, step = out_ref.shape[0], min(w_ref.shape[0], 256)
    own = pl.ds(pl.multiple_of(lax.axis_index("layer") * half, half), half)
    for i in range(w_ref.shape[0] // step):
        cols = slice(i * step, (i + 1) * step)
        out_ref[:, cols] = lax.dot_general(q_ref[own, :], w_ref[cols, :], NT, preferred_element_type=F32)


def last_kernel(masks, *refs):
    *groups, q_ref, first_ref, out_hbm, w_ref, out_ref, sems = refs
    arrange(masks, groups, w_ref)
    half, step, parts = first_ref.shape[0], min(w_ref.shape[0], 256), sems.shape[0]
    start, rows = lax.axis_index("layer") * half, half // parts
    copies = []
    for r in range(parts):
        own = pl.ds(pl.multiple_of(start + r * rows, rows), rows)
        here = pl.ds(r * rows, rows)
        for i in range(w_ref.shape[0] // step):
            cols = slice(i * step, (i + 1) * step)
            second = lax.dot_general(q_ref[own, :], w_ref[cols, :], NT, preferred_element_type=F32)
            out_ref[here, cols] = (first_ref[here, cols] + second).astype(BF16)
        copies.append(pltpu.make_async_copy(out_ref.at[here], out_hbm.at[here], sems.at[r]))
        copies[-1].start()
    for copy in copies:
        copy.wait()


def first_scores(masks, groups, queries):
    train, grad = sum(group.shape[0] for group in groups), queries.shape[1]
    half = queries.shape[0] // 2
    return pl.pallas_call(
        functools.partial(first_kernel, masks),
        out_shape=jax.ShapeDtypeStruct((half, train), F32),
        in_specs=[VMEM] * (len(groups) + 1),
        out_specs=VMEM,
        scratch_shapes=[pltpu.VMEM((train, grad), BF16)],
        compiler_params=PARAMS,
        cost_estimate=estimate(2 * train * grad * half, 2 * half * grad),
        name="first_scores",
    )(*groups, queries)


def last_scores(masks, groups, queries, first):
    train, grad = sum(group.shape[0] for group in groups), queries.shape[1]
    half = queries.shape[0] // 2
    return pl.pallas_call(
        functools.partial(last_kernel, masks),
        out_shape=jax.ShapeDtypeStruct((half, train), BF16),
        in_specs=[VMEM] * (len(groups) + 2),
        out_specs=HBM,
        scratch_shapes=[pltpu.VMEM((train, grad), BF16), pltpu.VMEM((half, train), BF16), pltpu.SemaphoreType.DMA((2,))],
        compiler_params=PARAMS,
        cost_estimate=estimate(2 * train * grad * half, 2 * half * grad),
        name="last_scores",
    )(*groups, queries, first)


def exchange(x, n, mask):
    return lax.ppermute(x, "pb", [(i, i ^ mask) for i in range(n)])


def other_layer(x):
    return lax.ppermute(x, "layer", [(0, 1), (1, 0)])


def on_device(n, query_grads, train_grads, basis_in, basis_out, eigenvalues):
    train = train_grads.reshape(train_grads.shape[0], -1)
    queries = query_grads.reshape(query_grads.shape[0], -1)
    other_queries = other_layer(queries)
    if n == 8:
        far = [exchange(train, n, mask) for mask in (4, 6)]
        last, _ = lax.optimization_barrier((train, other_queries))
        second, _ = lax.optimization_barrier((far[1], other_queries))
        near = [exchange(block, n, mask) for block, mask in ((train, 3), (train, 1), (last, 2))]
        groups, masks = [[train] + far + near, [exchange(block, n, 1) for block in (far[0], second)]], (0, 4, 6, 3, 1, 2, 5, 7)
        basis_in, basis_out, eigenvalues, _ = lax.optimization_barrier((basis_in, basis_out, eigenvalues, far[0]))
    else:
        groups, masks = [[lax.all_gather(train, "pb", axis=0, tiled=True)]], (0,)
    kron, inverse = kron_bases(basis_in, basis_out, eigenvalues)
    own = [precondition(groups[0], kron, inverse, "early_rows")]
    if len(groups) > 1:
        own[0], *late = lax.optimization_barrier([own[0]] + groups[1])
        own.append(precondition(late, kron, inverse, "late_rows"))
    other = [other_layer(w) for w in own]
    return last_scores(masks, other, other_queries, first_scores(masks, own, queries))


def solution(mesh):
    placed = (
        P(("grp", "pb"), "layer", None),
        P(("grp", "pb"), "layer", None),
        P("layer", None, None),
        P("layer", None, None),
        P("layer", None, None),
    )
    return jax.shard_map(
        functools.partial(on_device, mesh.shape["pb"]),
        mesh=mesh,
        in_specs=placed,
        out_specs=P(("grp", "pb", "layer"), None),
        check_vma=False,
    )
```

```python
import functools

import jax
import jax.numpy as jnp
from jax import lax
from jax.experimental import pallas as pl
from jax.experimental.pallas import tpu as pltpu
from jax.sharding import PartitionSpec as P

F32, BF16 = jnp.float32, jnp.bfloat16
VMEM = pl.BlockSpec(memory_space=pltpu.VMEM)
HBM = pl.BlockSpec(memory_space=pl.ANY)
HIGH = lax.Precision.HIGHEST
NT = (((1,), (1,)), ((), ()))
PARAMS = pltpu.CompilerParams(vmem_limit_bytes=24 * 1024 * 1024)


def estimate(flops, bytes_accessed):
    return pl.CostEstimate(flops=flops, bytes_accessed=bytes_accessed, transcendentals=0)


def kron_kernel(in_hbm, out_hbm, eigen_hbm, kron_ref, turned_ref, inverse_ref, basis_in, basis_out, eigen, sems):
    pairs = ((in_hbm, basis_in), (out_hbm, basis_out), (eigen_hbm, eigen))
    copies = [pltpu.make_async_copy(*pair, sems.at[i]) for i, pair in enumerate(pairs)]
    for copy in copies:
        copy.start()
    kout, kin = basis_out.shape[1], basis_in.shape[1]
    grad = kout * kin
    lane_out = lax.broadcasted_iota(jnp.int32, (kout, grad), 1) // kin
    repeat = (lax.broadcasted_iota(jnp.int32, (kout, grad), 0) == lane_out).astype(F32)
    lane_in = lax.broadcasted_iota(jnp.int32, (kin, grad), 1) % kin
    tile = (lax.broadcasted_iota(jnp.int32, (kin, grad), 0) == lane_in).astype(F32)
    for copy in copies:
        copy.wait()
    inner = jnp.concatenate([basis_in[0], basis_in[0].T, eigen[0]], axis=0)
    outer = jnp.concatenate([basis_out[0], basis_out[0].T], axis=0)
    tiled = jnp.dot(inner, tile, precision=HIGH, preferred_element_type=F32)
    spread = jnp.dot(outer, repeat, precision=HIGH, preferred_element_type=F32)
    tiled_in, turned_in, tiled_eigen = tiled[:kin], tiled[kin:2 * kin], tiled[2 * kin:]
    inverse_ref[...] = 1.0 / (jnp.sum(tiled_eigen * repeat, axis=0, keepdims=True) + 0.1)
    for b in range(kout):
        kron_ref[pl.ds(b * kin, kin), :] = (spread[b:b + 1, :] * tiled_in).astype(BF16)
        turned_ref[pl.ds(b * kin, kin), :] = (spread[kout + b:kout + b + 1, :] * turned_in).astype(BF16)


def kron_bases(basis_in, basis_out, eigenvalues):
    grad = basis_in.shape[1] * basis_out.shape[1]
    args = [pltpu.with_memory_space_constraint(x, pltpu.HBM) for x in (basis_in, basis_out, eigenvalues)]
    return pl.pallas_call(
        kron_kernel,
        out_shape=tuple(jax.ShapeDtypeStruct(*x) for x in (((grad, grad), BF16), ((grad, grad), BF16), ((1, grad), F32))),
        in_specs=[HBM] * 3,
        out_specs=(VMEM,) * 3,
        scratch_shapes=[pltpu.VMEM(x.shape, F32) for x in args] + [pltpu.SemaphoreType.DMA((3,))],
        compiler_params=PARAMS,
        cost_estimate=estimate(4 * grad**3, 0),
        name="kron_bases",
    )(*args)


def fill_rows(masks, blocks, kron_ref, turned_ref, inverse_ref, w_ref, rows_ref):
    size = blocks[0].shape[0]
    for i, block in enumerate(blocks):
        rows_ref[pl.ds(i * size, size), :] = block[...]
    total = len(blocks) * size
    step = min(total, 256)
    for i in range(total // step):
        rows = pl.ds(i * step, step)
        rotated = jnp.dot(rows_ref[rows, :], kron_ref[...], preferred_element_type=F32)
        scaled = (rotated * inverse_ref[...]).astype(BF16)
        rows_ref[rows, :] = jnp.dot(scaled, turned_ref[...], preferred_element_type=F32).astype(BF16)
    me = lax.axis_index("pb")
    for i, mask in enumerate(masks):
        at = pl.multiple_of((me ^ mask) * size, size) if len(masks) > 1 else 0
        w_ref[pl.ds(at, size), :] = rows_ref[pl.ds(i * size, size), :]


def score_half(layer, q_ref, w_ref, out_ref):
    half, step = out_ref.shape[0], min(w_ref.shape[0], 256)
    rows = pl.ds(pl.multiple_of(layer * half, half), half)
    for i in range(w_ref.shape[0] // step):
        cols = slice(i * step, (i + 1) * step)
        product = lax.dot_general(q_ref[rows, :], w_ref[cols, :], NT, preferred_element_type=F32)
        out_ref[:, cols] = product.astype(out_ref.dtype)


def early_kernel(masks, *refs):
    *blocks, kron_ref, turned_ref, inverse_ref, w_ref, rows_ref = refs
    fill_rows(masks, blocks, kron_ref, turned_ref, inverse_ref, w_ref, rows_ref)


def late_kernel(masks, *refs):
    *blocks, kron_ref, turned_ref, inverse_ref, _, q_ref, w_ref, out_ref, rows_ref = refs
    if blocks:
        fill_rows(masks, blocks, kron_ref, turned_ref, inverse_ref, w_ref, rows_ref)
    score_half(1 - lax.axis_index("layer"), q_ref, w_ref, out_ref)


def own_kernel(w_ref, q_ref, out_ref):
    score_half(lax.axis_index("layer"), q_ref, w_ref, out_ref)


def early_rows(masks, blocks, bases, train):
    rows, grad = sum(block.shape[0] for block in blocks), bases[0].shape[0]
    return pl.pallas_call(
        functools.partial(early_kernel, masks),
        out_shape=jax.ShapeDtypeStruct((train, grad), BF16),
        in_specs=[VMEM] * (len(blocks) + 3),
        out_specs=VMEM,
        scratch_shapes=[pltpu.VMEM((rows, grad), BF16)],
        compiler_params=PARAMS,
        cost_estimate=estimate(0, 0),
        name="early_rows",
    )(*blocks, *bases)


def outgoing_scores(masks, blocks, bases, w, queries):
    rows, (train, grad), half = sum(block.shape[0] for block in blocks), w.shape, queries.shape[0] // 2
    return pl.pallas_call(
        functools.partial(late_kernel, masks),
        out_shape=(jax.ShapeDtypeStruct((train, grad), BF16), jax.ShapeDtypeStruct((half, train), BF16)),
        in_specs=[VMEM] * (len(blocks) + 5),
        out_specs=(VMEM, VMEM),
        input_output_aliases={len(blocks) + 3: 0},
        scratch_shapes=[pltpu.VMEM((max(rows, 32), grad), BF16)],
        compiler_params=PARAMS,
        cost_estimate=estimate(2 * train * grad * half, 2 * half * grad),
        name="outgoing_scores",
    )(*blocks, *bases, w, queries)


def own_scores(w, queries):
    (train, grad), half = w.shape, queries.shape[0] // 2
    return pl.pallas_call(
        own_kernel,
        out_shape=jax.ShapeDtypeStruct((half, train), F32),
        in_specs=[VMEM, VMEM],
        out_specs=VMEM,
        compiler_params=PARAMS,
        cost_estimate=estimate(2 * train * grad * half, 2 * half * grad),
        name="own_scores",
    )(w, queries)


def add_kernel(own_ref, received_ref, out_hbm, out_ref, sems):
    rows = own_ref.shape[0] // sems.shape[0]
    copies = []
    for i in range(sems.shape[0]):
        here = pl.ds(i * rows, rows)
        out_ref[here, :] = (own_ref[here, :] + received_ref[here, :].astype(F32)).astype(BF16)
        copies.append(pltpu.make_async_copy(out_ref.at[here], out_hbm.at[here], sems.at[i]))
        copies[-1].start()
    for copy in copies:
        copy.wait()


def add_scores(own, received):
    return pl.pallas_call(
        add_kernel,
        out_shape=jax.ShapeDtypeStruct(own.shape, BF16),
        in_specs=[VMEM, VMEM],
        out_specs=HBM,
        scratch_shapes=[pltpu.VMEM(own.shape, BF16), pltpu.SemaphoreType.DMA((4,))],
        compiler_params=PARAMS,
        cost_estimate=estimate(0, 0),
        name="add_scores",
    )(own, received)


def exchange(x, n, mask):
    return lax.ppermute(x, "pb", [(i, i ^ mask) for i in range(n)])


def on_device(n, query_grads, train_grads, basis_in, basis_out, eigenvalues):
    train = train_grads.reshape(train_grads.shape[0], -1)
    queries = query_grads.reshape(query_grads.shape[0], -1)
    if n == 8:
        far = [exchange(train, n, mask) for mask in (4, 6)]
        near = [exchange(train, n, mask) for mask in (2, 1, 3)]
        early, late = [train] + far + near, [exchange(block, n, 1) for block in far]
        early_masks, late_masks = (0, 4, 6, 2, 1, 3), (5, 7)
        basis_in, basis_out, eigenvalues, _ = lax.optimization_barrier((basis_in, basis_out, eigenvalues, far[0]))
    else:
        early, late = [lax.all_gather(train, "pb", axis=0, tiled=True)], []
        early_masks, late_masks = (0,), ()
    bases = kron_bases(basis_in, basis_out, eigenvalues)
    w = early_rows(early_masks, early, bases, n * train.shape[0])
    w, sent = outgoing_scores(late_masks, late, bases, w, queries)
    received = lax.ppermute(sent, "layer", [(0, 1), (1, 0)])
    return add_scores(own_scores(w, queries), received)


def solution(mesh):
    placed = (
        P(("grp", "pb"), "layer", None),
        P(("grp", "pb"), "layer", None),
        P("layer", None, None),
        P("layer", None, None),
        P("layer", None, None),
    )
    return jax.shard_map(
        functools.partial(on_device, mesh.shape["pb"]),
        mesh=mesh,
        in_specs=placed,
        out_specs=P(("grp", "pb", "layer"), None),
        check_vma=False,
    )
```

```python
import functools

import jax
import jax.numpy as jnp
from jax import lax
from jax.experimental import pallas as pl
from jax.experimental.pallas import tpu as pltpu
from jax.sharding import PartitionSpec as P

F32, BF16 = jnp.float32, jnp.bfloat16
VMEM = pl.BlockSpec(memory_space=pltpu.VMEM)
HBM = pl.BlockSpec(memory_space=pl.ANY)
NT = (((1,), (1,)), ((), ()))
PARAMS = pltpu.CompilerParams(vmem_limit_bytes=24 * 1024 * 1024)


def estimate(flops, bytes_accessed):
    return pl.CostEstimate(flops=flops, bytes_accessed=bytes_accessed, transcendentals=0)


def selector_kernel(kin, chosen_ref):
    kout, grad = chosen_ref.shape[0] - kin, chosen_ref.shape[1]
    lane = lax.broadcasted_iota(jnp.int32, (kout, grad), 1)
    chosen_ref[:kout, :] = (lax.broadcasted_iota(jnp.int32, (kout, grad), 0) == lane // kin).astype(F32).astype(BF16)
    lane = lax.broadcasted_iota(jnp.int32, (kin, grad), 1)
    chosen_ref[kout:, :] = (lax.broadcasted_iota(jnp.int32, (kin, grad), 0) == lane % kin).astype(F32).astype(BF16)


def selectors(kout, kin):
    return pl.pallas_call(
        functools.partial(selector_kernel, kin),
        out_shape=jax.ShapeDtypeStruct((kout + kin, kout * kin), BF16),
        out_specs=VMEM,
        compiler_params=PARAMS,
        cost_estimate=estimate(2 * (kout * kin)**3, 0),
        name="selectors",
    )()


def select(matrices, chosen):
    rest, parts = jnp.concatenate(matrices, axis=0), []
    for _ in range(3):
        parts.append(rest.astype(BF16))
        rest = rest - parts[-1].astype(F32)
    product = jnp.dot(jnp.concatenate(parts, axis=0), chosen, preferred_element_type=F32)
    rows = rest.shape[0]
    return product[:rows] + product[rows:2 * rows] + product[2 * rows:]


def kron_kernel(basis_in, basis_out, eigen, chosen_ref, _, kron_ref, turned_ref, inverse_ref):
    kout, kin = basis_out.shape[1], basis_in.shape[1]
    repeat, tile = chosen_ref[:kout, :], chosen_ref[kout:, :]
    tiled = select([basis_in[0], basis_in[0].T, eigen[0]], tile)
    spread = select([basis_out[0], basis_out[0].T], repeat)
    tiled_in, turned_in, tiled_eigen = tiled[:kin], tiled[kin:2 * kin], tiled[2 * kin:]
    inverse_ref[...] = 1.0 / (jnp.sum(tiled_eigen * repeat.astype(F32), axis=0, keepdims=True) + 0.1)
    for b in range(kout):
        kron_ref[pl.ds(b * kin, kin), :] = (spread[b:b + 1, :] * tiled_in).astype(BF16)
    for a in range(kout):
        turned_ref[pl.ds(a * kin, kin), :] = (spread[kout + a:kout + a + 1, :] * turned_in).astype(BF16)


def kron_bases(basis_in, basis_out, eigenvalues, chosen, queries):
    grad = chosen.shape[1]
    return pl.pallas_call(
        kron_kernel,
        out_shape=tuple(jax.ShapeDtypeStruct(*x) for x in (((grad, grad), BF16), ((grad, grad), BF16), ((1, grad), F32))),
        in_specs=[VMEM] * 5,
        out_specs=(VMEM,) * 3,
        compiler_params=PARAMS,
        cost_estimate=estimate(4 * grad**3, 0),
        name="kron_bases",
    )(basis_in, basis_out, eigenvalues, chosen, queries)


def fill_rows(masks, blocks, kron_ref, turned_ref, inverse_ref, w_ref, rows_ref):
    size = blocks[0].shape[0]
    for i, block in enumerate(blocks):
        rows_ref[pl.ds(i * size, size), :] = block[...]
    total = len(blocks) * size
    step = min(total, 256)
    for i in range(total // step):
        rows = pl.ds(i * step, step)
        rotated = jnp.dot(rows_ref[rows, :], kron_ref[...], preferred_element_type=F32)
        scaled = (rotated * inverse_ref[...]).astype(BF16)
        rows_ref[rows, :] = jnp.dot(scaled, turned_ref[...], preferred_element_type=F32).astype(BF16)
    me = lax.axis_index("pb")
    for i, mask in enumerate(masks):
        at = pl.multiple_of((me ^ mask) * size, size) if len(masks) > 1 else 0
        w_ref[pl.ds(at, size), :] = rows_ref[pl.ds(i * size, size), :]


def score_half(layer, q_ref, w_ref, out_ref):
    half, step = out_ref.shape[0], min(w_ref.shape[0], 256)
    rows = pl.ds(pl.multiple_of(layer * half, half), half)
    for i in range(w_ref.shape[0] // step):
        cols = slice(i * step, (i + 1) * step)
        product = lax.dot_general(q_ref[rows, :], w_ref[cols, :], NT, preferred_element_type=F32)
        out_ref[:, cols] = product.astype(out_ref.dtype)


def early_kernel(masks, *refs):
    *blocks, kron_ref, turned_ref, inverse_ref, w_ref, rows_ref = refs
    fill_rows(masks, blocks, kron_ref, turned_ref, inverse_ref, w_ref, rows_ref)


def late_kernel(masks, *refs):
    *blocks, kron_ref, turned_ref, inverse_ref, _, q_ref, w_ref, out_ref, rows_ref = refs
    if blocks:
        fill_rows(masks, blocks, kron_ref, turned_ref, inverse_ref, w_ref, rows_ref)
    score_half(1 - lax.axis_index("layer"), q_ref, w_ref, out_ref)


def own_kernel(w_ref, q_ref, out_ref):
    score_half(lax.axis_index("layer"), q_ref, w_ref, out_ref)


def early_rows(masks, blocks, bases, train):
    rows, grad = sum(block.shape[0] for block in blocks), bases[0].shape[0]
    return pl.pallas_call(
        functools.partial(early_kernel, masks),
        out_shape=jax.ShapeDtypeStruct((train, grad), BF16),
        in_specs=[VMEM] * (len(blocks) + 3),
        out_specs=VMEM,
        scratch_shapes=[pltpu.VMEM((rows, grad), BF16)],
        compiler_params=PARAMS,
        cost_estimate=estimate(0, 0),
        name="early_rows",
    )(*blocks, *bases)


def outgoing_scores(masks, blocks, bases, w, queries):
    rows, (train, grad), half = sum(block.shape[0] for block in blocks), w.shape, queries.shape[0] // 2
    return pl.pallas_call(
        functools.partial(late_kernel, masks),
        out_shape=(jax.ShapeDtypeStruct((train, grad), BF16), jax.ShapeDtypeStruct((half, train), BF16)),
        in_specs=[VMEM] * (len(blocks) + 5),
        out_specs=(VMEM, VMEM),
        input_output_aliases={len(blocks) + 3: 0},
        scratch_shapes=[pltpu.VMEM((max(rows, 32), grad), BF16)],
        compiler_params=PARAMS,
        cost_estimate=estimate(2 * train * grad * half, 2 * half * grad),
        name="outgoing_scores",
    )(*blocks, *bases, w, queries)


def own_scores(w, queries):
    (train, grad), half = w.shape, queries.shape[0] // 2
    return pl.pallas_call(
        own_kernel,
        out_shape=jax.ShapeDtypeStruct((half, train), F32),
        in_specs=[VMEM, VMEM],
        out_specs=VMEM,
        compiler_params=PARAMS,
        cost_estimate=estimate(2 * train * grad * half, 2 * half * grad),
        name="own_scores",
    )(w, queries)


def add_kernel(own_ref, received_ref, out_hbm, out_ref, sems):
    rows = own_ref.shape[0] // sems.shape[0]
    copies = []
    for i in range(sems.shape[0]):
        here = pl.ds(i * rows, rows)
        out_ref[here, :] = (own_ref[here, :] + received_ref[here, :].astype(F32)).astype(BF16)
        copies.append(pltpu.make_async_copy(out_ref.at[here], out_hbm.at[here], sems.at[i]))
        copies[-1].start()
    for copy in copies:
        copy.wait()


def add_scores(own, received):
    return pl.pallas_call(
        add_kernel,
        out_shape=jax.ShapeDtypeStruct(own.shape, BF16),
        in_specs=[VMEM, VMEM],
        out_specs=HBM,
        scratch_shapes=[pltpu.VMEM(own.shape, BF16), pltpu.SemaphoreType.DMA((4,))],
        compiler_params=PARAMS,
        cost_estimate=estimate(0, 0),
        name="add_scores",
    )(own, received)


def exchange(x, n, mask):
    return lax.ppermute(x, "pb", [(i, i ^ mask) for i in range(n)])


def on_device(n, query_grads, train_grads, basis_in, basis_out, eigenvalues):
    train = train_grads.reshape(train_grads.shape[0], -1)
    queries = query_grads.reshape(query_grads.shape[0], -1)
    chosen = selectors(basis_out.shape[1], basis_in.shape[1])
    if n == 8:
        far = [exchange(train, n, mask) for mask in (6, 4)]
        behind, chosen = lax.optimization_barrier((train, chosen))
        near = [exchange(behind, n, mask) for mask in (2, 1, 3)]
        early, late = [train] + far + near, [exchange(block, n, 1) for block in far]
        early_masks, late_masks = (0, 6, 4, 2, 1, 3), (7, 5)
    else:
        early, late = [lax.all_gather(train, "pb", axis=0, tiled=True)], []
        early_masks, late_masks = (0,), ()
    bases = kron_bases(basis_in, basis_out, eigenvalues, chosen, queries)
    w = early_rows(early_masks, early, bases, n * train.shape[0])
    w, sent = outgoing_scores(late_masks, late, bases, w, queries)
    received = lax.ppermute(sent, "layer", [(0, 1), (1, 0)])
    return add_scores(own_scores(w, queries), received)


def solution(mesh):
    placed = (
        P(("grp", "pb"), "layer", None),
        P(("grp", "pb"), "layer", None),
        P("layer", None, None),
        P("layer", None, None),
        P("layer", None, None),
    )
    return jax.shard_map(
        functools.partial(on_device, mesh.shape["pb"]),
        mesh=mesh,
        in_specs=placed,
        out_specs=P(("grp", "pb", "layer"), None),
        check_vma=False,
    )
```

```python
import functools

import jax
import jax.numpy as jnp
from jax import lax
from jax.experimental import pallas as pl
from jax.experimental.pallas import tpu as pltpu
from jax.sharding import PartitionSpec as P

F32, BF16 = jnp.float32, jnp.bfloat16
VMEM = pl.BlockSpec(memory_space=pltpu.VMEM)
HBM = pl.BlockSpec(memory_space=pl.ANY)
NT = (((1,), (1,)), ((), ()))
PARAMS = pltpu.CompilerParams(vmem_limit_bytes=24 * 1024 * 1024)


def estimate(flops, bytes_accessed):
    return pl.CostEstimate(flops=flops, bytes_accessed=bytes_accessed, transcendentals=0)


def selector_kernel(kin, chosen_ref):
    kout, grad = chosen_ref.shape[0] - kin, chosen_ref.shape[1]
    lane = lax.broadcasted_iota(jnp.int32, (kout, grad), 1)
    chosen_ref[:kout, :] = (lax.broadcasted_iota(jnp.int32, (kout, grad), 0) == lane // kin).astype(F32).astype(BF16)
    lane = lax.broadcasted_iota(jnp.int32, (kin, grad), 1)
    chosen_ref[kout:, :] = (lax.broadcasted_iota(jnp.int32, (kin, grad), 0) == lane % kin).astype(F32).astype(BF16)


def selectors(kout, kin):
    return pl.pallas_call(
        functools.partial(selector_kernel, kin),
        out_shape=jax.ShapeDtypeStruct((kout + kin, kout * kin), BF16),
        out_specs=VMEM,
        compiler_params=PARAMS,
        cost_estimate=estimate(2 * (kout * kin)**3, 0),
        name="selectors",
    )()


def select(matrices, chosen):
    rest, parts = jnp.concatenate(matrices, axis=0), []
    for _ in range(3):
        parts.append(rest.astype(BF16))
        rest = rest - parts[-1].astype(F32)
    product = jnp.dot(jnp.concatenate(parts, axis=0), chosen, preferred_element_type=F32)
    rows = rest.shape[0]
    return product[:rows] + product[rows:2 * rows] + product[2 * rows:]


def kron_kernel(basis_in, basis_out, eigen, chosen_ref, _, kron_ref, turned_ref, inverse_ref):
    kout, kin = basis_out.shape[1], basis_in.shape[1]
    repeat, tile = chosen_ref[:kout, :], chosen_ref[kout:, :]
    tiled = select([basis_in[0], basis_in[0].T, eigen[0]], tile)
    spread = select([basis_out[0], basis_out[0].T], repeat)
    tiled_in, turned_in, tiled_eigen = tiled[:kin], tiled[kin:2 * kin], tiled[2 * kin:]
    inverse_ref[...] = 1.0 / (jnp.sum(tiled_eigen * repeat.astype(F32), axis=0, keepdims=True) + 0.1)
    for b in range(kout):
        kron_ref[pl.ds(b * kin, kin), :] = (spread[b:b + 1, :] * tiled_in).astype(BF16)
    for a in range(kout):
        turned_ref[pl.ds(a * kin, kin), :] = (spread[kout + a:kout + a + 1, :] * turned_in).astype(BF16)


def kron_bases(basis_in, basis_out, eigenvalues, chosen, queries):
    grad = chosen.shape[1]
    return pl.pallas_call(
        kron_kernel,
        out_shape=tuple(jax.ShapeDtypeStruct(*x) for x in (((grad, grad), BF16), ((grad, grad), BF16), ((1, grad), F32))),
        in_specs=[VMEM] * 5,
        out_specs=(VMEM,) * 3,
        compiler_params=PARAMS,
        cost_estimate=estimate(grad**3 // 2, 0),
        name="kron_bases",
    )(basis_in, basis_out, eigenvalues, chosen, queries)


def precondition_kernel(*refs):
    *blocks, kron_ref, turned_ref, inverse_ref, w_ref = refs
    size, total = blocks[0].shape[0], w_ref.shape[0]
    for i, block in enumerate(blocks):
        w_ref[pl.ds(i * size, size), :] = block[...]
    step = min(total, 256)
    for i in range(total // step):
        rows = pl.ds(i * step, step)
        rotated = jnp.dot(w_ref[rows, :], kron_ref[...], preferred_element_type=F32)
        scaled = (rotated * inverse_ref[...]).astype(BF16)
        w_ref[rows, :] = jnp.dot(scaled, turned_ref[...], preferred_element_type=F32).astype(BF16)


def precondition(blocks, bases, name):
    rows, grad = sum(block.shape[0] for block in blocks), bases[0].shape[0]
    return pl.pallas_call(
        precondition_kernel,
        out_shape=jax.ShapeDtypeStruct((rows, grad), BF16),
        in_specs=[VMEM] * (len(blocks) + 3),
        out_specs=VMEM,
        compiler_params=PARAMS,
        cost_estimate=estimate((0 if name == "early_rows" else int(19.5 * grad**3)), 0),
        name=name,
    )(*blocks, *bases)


def arrange(masks, groups, w_ref):
    me, size = lax.axis_index("pb"), w_ref.shape[0] // len(masks)
    i = 0
    for group in groups:
        for row in range(0, group.shape[0], size):
            at = pl.multiple_of((me ^ masks[i]) * size, size) if len(masks) > 1 else 0
            w_ref[pl.ds(at, size), :] = group[pl.ds(row, size), :]
            i += 1


def first_kernel(masks, *refs):
    *groups, q_ref, out_ref, w_ref = refs
    arrange(masks, groups, w_ref)
    half, step = out_ref.shape[0], min(w_ref.shape[0], 256)
    own = pl.ds(pl.multiple_of(lax.axis_index("layer") * half, half), half)
    for i in range(w_ref.shape[0] // step):
        cols = slice(i * step, (i + 1) * step)
        out_ref[:, cols] = lax.dot_general(q_ref[own, :], w_ref[cols, :], NT, preferred_element_type=F32)


def last_kernel(masks, *refs):
    *groups, q_ref, first_ref, out_hbm, w_ref, out_ref, sems = refs
    arrange(masks, groups, w_ref)
    half, step, parts = first_ref.shape[0], min(w_ref.shape[0], 256), sems.shape[0]
    rows = half // parts
    copies = []
    for r in range(parts):
        here = pl.ds(r * rows, rows)
        for i in range(w_ref.shape[0] // step):
            cols = slice(i * step, (i + 1) * step)
            second = lax.dot_general(q_ref[here, :], w_ref[cols, :], NT, preferred_element_type=F32)
            out_ref[here, cols] = (first_ref[here, cols] + second).astype(BF16)
        copies.append(pltpu.make_async_copy(out_ref.at[here], out_hbm.at[here], sems.at[r]))
        copies[-1].start()
    for copy in copies:
        copy.wait()


def first_scores(masks, groups, queries):
    train, grad = sum(group.shape[0] for group in groups), queries.shape[1]
    half = queries.shape[0] // 2
    return pl.pallas_call(
        functools.partial(first_kernel, masks),
        out_shape=jax.ShapeDtypeStruct((half, train), F32),
        in_specs=[VMEM] * (len(groups) + 1),
        out_specs=VMEM,
        scratch_shapes=[pltpu.VMEM((train, grad), BF16)],
        compiler_params=PARAMS,
        cost_estimate=estimate(2 * train * grad * half, 2 * half * grad),
        name="first_scores",
    )(*groups, queries)


def last_scores(masks, groups, queries, first):
    train, grad = sum(group.shape[0] for group in groups), queries.shape[1]
    half = queries.shape[0]
    return pl.pallas_call(
        functools.partial(last_kernel, masks),
        out_shape=jax.ShapeDtypeStruct((half, train), BF16),
        in_specs=[VMEM] * (len(groups) + 2),
        out_specs=HBM,
        scratch_shapes=[pltpu.VMEM((train, grad), BF16), pltpu.VMEM((half, train), BF16), pltpu.SemaphoreType.DMA((2,))],
        compiler_params=PARAMS,
        cost_estimate=estimate(2 * train * grad * half, 2 * half * grad),
        name="last_scores",
    )(*groups, queries, first)


def theirs_kernel(q_ref, theirs_ref):
    half = theirs_ref.shape[0]
    start, rows = (1 - lax.axis_index("layer")) * half, min(half, 256)
    for i in range(half // rows):
        there = pl.ds(pl.multiple_of(start + i * rows, rows), rows)
        theirs_ref[pl.ds(i * rows, rows), :] = q_ref[there, :]


def other_half(queries):
    rows, grad = queries.shape
    return pl.pallas_call(
        theirs_kernel,
        out_shape=jax.ShapeDtypeStruct((rows // 2, grad), BF16),
        in_specs=[VMEM],
        out_specs=VMEM,
        compiler_params=PARAMS,
        cost_estimate=estimate(4 * grad**3, 0),
        name="other_half",
    )(queries)


def exchange(x, n, mask):
    return lax.ppermute(x, "pb", [(i, i ^ mask) for i in range(n)])


def other_layer(x):
    return lax.ppermute(x, "layer", [(0, 1), (1, 0)])


def on_device(n, query_grads, train_grads, basis_in, basis_out, eigenvalues):
    train = train_grads.reshape(train_grads.shape[0], -1)
    queries = query_grads.reshape(query_grads.shape[0], -1)
    chosen = selectors(basis_out.shape[1], basis_in.shape[1])
    if n == 8:
        far = [exchange(train, n, mask) for mask in (4, 6)]
        behind, chosen = lax.optimization_barrier((train, chosen))
        near = [exchange(behind, n, mask) for mask in (2, 1, 3)]
        groups, masks = [[train] + far + near, [exchange(block, n, 1) for block in far]], (0, 4, 6, 2, 1, 3, 5, 7)
        loose, *_ = lax.optimization_barrier([queries] + [])
        sent = other_half(loose)
        sent, *_ = lax.optimization_barrier([sent] + near[1:2])
    else:
        groups, masks = [[lax.all_gather(train, "pb", axis=0, tiled=True)]], (0,)
        sent = other_half(queries)
    other_queries = other_layer(sent)
    bases = kron_bases(basis_in, basis_out, eigenvalues, chosen, queries)
    own = [precondition(groups[0], bases, "early_rows")]
    if len(groups) > 1:
        own[0], *groups[1] = lax.optimization_barrier([own[0]] + groups[1])
        own.append(precondition(groups[1], bases, "late_rows"))
    other = [other_layer(w) for w in own]
    return last_scores(masks, other, other_queries, first_scores(masks, own, queries))


def solution(mesh):
    placed = (
        P(("grp", "pb"), "layer", None),
        P(("grp", "pb"), "layer", None),
        P("layer", None, None),
        P("layer", None, None),
        P("layer", None, None),
    )
    return jax.shard_map(
        functools.partial(on_device, mesh.shape["pb"]),
        mesh=mesh,
        in_specs=placed,
        out_specs=P(("grp", "pb", "layer"), None),
        check_vma=False,
    )
```

```python
import functools

import jax
import jax.numpy as jnp
from jax import lax
from jax.experimental import pallas as pl
from jax.experimental.pallas import tpu as pltpu
from jax.sharding import PartitionSpec as P

F32, BF16 = jnp.float32, jnp.bfloat16
VMEM = pl.BlockSpec(memory_space=pltpu.VMEM)
HBM = pl.BlockSpec(memory_space=pl.ANY)
NT = (((1,), (1,)), ((), ()))
PARAMS = pltpu.CompilerParams(vmem_limit_bytes=24 * 1024 * 1024)


def estimate(flops, bytes_accessed):
    return pl.CostEstimate(flops=flops, bytes_accessed=bytes_accessed, transcendentals=0)


def selector_kernel(kin, chosen_ref):
    kout, grad = chosen_ref.shape[0] - kin, chosen_ref.shape[1]
    lane = lax.broadcasted_iota(jnp.int32, (kout, grad), 1)
    chosen_ref[:kout, :] = (lax.broadcasted_iota(jnp.int32, (kout, grad), 0) == lane // kin).astype(F32).astype(BF16)
    lane = lax.broadcasted_iota(jnp.int32, (kin, grad), 1)
    chosen_ref[kout:, :] = (lax.broadcasted_iota(jnp.int32, (kin, grad), 0) == lane % kin).astype(F32).astype(BF16)


def selectors(kout, kin):
    return pl.pallas_call(
        functools.partial(selector_kernel, kin),
        out_shape=jax.ShapeDtypeStruct((kout + kin, kout * kin), BF16),
        out_specs=VMEM,
        compiler_params=PARAMS,
        cost_estimate=estimate(2 * (kout * kin)**3, 0),
        name="selectors",
    )()


def select(matrices, chosen):
    rest, parts = jnp.concatenate(matrices, axis=0), []
    for _ in range(3):
        parts.append(rest.astype(BF16))
        rest = rest - parts[-1].astype(F32)
    product = jnp.dot(jnp.concatenate(parts, axis=0), chosen, preferred_element_type=F32)
    rows = rest.shape[0]
    return product[:rows] + product[rows:2 * rows] + product[2 * rows:]


def kron_kernel(basis_in, basis_out, eigen, chosen_ref, _, kron_ref, turned_ref, inverse_ref):
    kout, kin = basis_out.shape[1], basis_in.shape[1]
    repeat, tile = chosen_ref[:kout, :], chosen_ref[kout:, :]
    tiled = select([basis_in[0], basis_in[0].T, eigen[0]], tile)
    spread = select([basis_out[0], basis_out[0].T], repeat)
    tiled_in, turned_in, tiled_eigen = tiled[:kin], tiled[kin:2 * kin], tiled[2 * kin:]
    inverse_ref[...] = 1.0 / (jnp.sum(tiled_eigen * repeat.astype(F32), axis=0, keepdims=True) + 0.1)
    for b in range(kout):
        kron_ref[pl.ds(b * kin, kin), :] = (spread[b:b + 1, :] * tiled_in).astype(BF16)
    for a in range(kout):
        turned_ref[pl.ds(a * kin, kin), :] = (spread[kout + a:kout + a + 1, :] * turned_in).astype(BF16)


def kron_bases(basis_in, basis_out, eigenvalues, chosen, queries):
    grad = chosen.shape[1]
    return pl.pallas_call(
        kron_kernel,
        out_shape=tuple(jax.ShapeDtypeStruct(*x) for x in (((grad, grad), BF16), ((grad, grad), BF16), ((1, grad), F32))),
        in_specs=[VMEM] * 5,
        out_specs=(VMEM,) * 3,
        compiler_params=PARAMS,
        cost_estimate=estimate(grad**3 // 2, 0),
        name="kron_bases",
    )(basis_in, basis_out, eigenvalues, chosen, queries)


def precondition_kernel(*refs):
    *blocks, kron_ref, turned_ref, inverse_ref, w_ref = refs
    size, total = blocks[0].shape[0], w_ref.shape[0]
    for i, block in enumerate(blocks):
        w_ref[pl.ds(i * size, size), :] = block[...]
    step = min(total, 256)
    for i in range(total // step):
        rows = pl.ds(i * step, step)
        rotated = jnp.dot(w_ref[rows, :], kron_ref[...], preferred_element_type=F32)
        scaled = (rotated * inverse_ref[...]).astype(BF16)
        w_ref[rows, :] = jnp.dot(scaled, turned_ref[...], preferred_element_type=F32).astype(BF16)


def precondition(blocks, bases, name):
    rows, grad = sum(block.shape[0] for block in blocks), bases[0].shape[0]
    return pl.pallas_call(
        precondition_kernel,
        out_shape=jax.ShapeDtypeStruct((rows, grad), BF16),
        in_specs=[VMEM] * (len(blocks) + 3),
        out_specs=VMEM,
        compiler_params=PARAMS,
        cost_estimate=estimate((0 if name == "early_rows" else int(19.5 * grad**3)), 0),
        name=name,
    )(*blocks, *bases)


def arrange(masks, groups, w_ref):
    me, size = lax.axis_index("pb"), w_ref.shape[0] // len(masks)
    i = 0
    for group in groups:
        for row in range(0, group.shape[0], size):
            at = pl.multiple_of((me ^ masks[i]) * size, size) if len(masks) > 1 else 0
            w_ref[pl.ds(at, size), :] = group[pl.ds(row, size), :]
            i += 1


def first_kernel(masks, *refs):
    *groups, q_ref, out_ref, w_ref = refs
    arrange(masks, groups, w_ref)
    half, step = out_ref.shape[0], min(w_ref.shape[0], 256)
    own = pl.ds(pl.multiple_of(lax.axis_index("layer") * half, half), half)
    for i in range(w_ref.shape[0] // step):
        cols = slice(i * step, (i + 1) * step)
        out_ref[:, cols] = lax.dot_general(q_ref[own, :], w_ref[cols, :], NT, preferred_element_type=F32)


def last_kernel(masks, *refs):
    *groups, q_ref, first_ref, out_hbm, w_ref, out_ref, sems = refs
    arrange(masks, groups, w_ref)
    half, train, parts = first_ref.shape[0], w_ref.shape[0], sems.shape[0]
    step, rows = min(train, 256), half // parts
    copies = []
    for i in range(train // step):
        cols = slice(i * step, (i + 1) * step)
        second = lax.dot_general(q_ref[...], w_ref[cols, :], NT, preferred_element_type=F32)
        for r in range(parts):
            here = slice(r * rows, (r + 1) * rows)
            out_ref[here, cols] = (first_ref[here, cols] + second[here]).astype(BF16)
            if (i + 1) * step == train:
                copies.append(pltpu.make_async_copy(out_ref.at[here], out_hbm.at[here], sems.at[r]))
                copies[-1].start()
    for copy in copies:
        copy.wait()


def first_scores(masks, groups, queries):
    train, grad = sum(group.shape[0] for group in groups), queries.shape[1]
    half = queries.shape[0] // 2
    return pl.pallas_call(
        functools.partial(first_kernel, masks),
        out_shape=jax.ShapeDtypeStruct((half, train), F32),
        in_specs=[VMEM] * (len(groups) + 1),
        out_specs=VMEM,
        scratch_shapes=[pltpu.VMEM((train, grad), BF16)],
        compiler_params=PARAMS,
        cost_estimate=estimate(2 * train * grad * half, 2 * half * grad),
        name="first_scores",
    )(*groups, queries)


def last_scores(masks, groups, queries, first):
    train, grad = sum(group.shape[0] for group in groups), queries.shape[1]
    half = queries.shape[0]
    return pl.pallas_call(
        functools.partial(last_kernel, masks),
        out_shape=jax.ShapeDtypeStruct((half, train), BF16),
        in_specs=[VMEM] * (len(groups) + 2),
        out_specs=HBM,
        scratch_shapes=[pltpu.VMEM((train, grad), BF16), pltpu.VMEM((half, train), BF16), pltpu.SemaphoreType.DMA((8,))],
        compiler_params=PARAMS,
        cost_estimate=estimate(2 * train * grad * half, 2 * half * grad),
        name="last_scores",
    )(*groups, queries, first)


def theirs_kernel(q_ref, theirs_ref):
    half = theirs_ref.shape[0]
    start, rows = (1 - lax.axis_index("layer")) * half, min(half, 256)
    for i in range(half // rows):
        there = pl.ds(pl.multiple_of(start + i * rows, rows), rows)
        theirs_ref[pl.ds(i * rows, rows), :] = q_ref[there, :]


def other_half(queries):
    rows, grad = queries.shape
    return pl.pallas_call(
        theirs_kernel,
        out_shape=jax.ShapeDtypeStruct((rows // 2, grad), BF16),
        in_specs=[VMEM],
        out_specs=VMEM,
        compiler_params=PARAMS,
        cost_estimate=estimate(4 * grad**3, 0),
        name="other_half",
    )(queries)


def exchange(x, n, mask):
    return lax.ppermute(x, "pb", [(i, i ^ mask) for i in range(n)])


def other_layer(x):
    return lax.ppermute(x, "layer", [(0, 1), (1, 0)])


def on_device(n, query_grads, train_grads, basis_in, basis_out, eigenvalues):
    train = train_grads.reshape(train_grads.shape[0], -1)
    queries = query_grads.reshape(query_grads.shape[0], -1)
    chosen = selectors(basis_out.shape[1], basis_in.shape[1])
    if n == 8:
        far = [exchange(train, n, mask) for mask in (4, 6)]
        behind, chosen = lax.optimization_barrier((train, chosen))
        near = [exchange(behind, n, mask) for mask in (2, 1, 3)]
        groups, masks = [[train] + far + near, [exchange(block, n, 1) for block in far]], (0, 4, 6, 2, 1, 3, 5, 7)
        loose, = lax.optimization_barrier((queries,))
        sent, _ = lax.optimization_barrier((other_half(loose), near[1]))
    else:
        groups, masks = [[lax.all_gather(train, "pb", axis=0, tiled=True)]], (0,)
        sent = other_half(queries)
    other_queries = other_layer(sent)
    bases = kron_bases(basis_in, basis_out, eigenvalues, chosen, queries)
    own = [precondition(groups[0], bases, "early_rows")]
    if len(groups) > 1:
        own[0], *groups[1] = lax.optimization_barrier([own[0]] + groups[1])
        own.append(precondition(groups[1], bases, "late_rows"))
    other = [other_layer(w) for w in own]
    return last_scores(masks, other, other_queries, first_scores(masks, own, queries))


def solution(mesh):
    placed = (
        P(("grp", "pb"), "layer", None),
        P(("grp", "pb"), "layer", None),
        P("layer", None, None),
        P("layer", None, None),
        P("layer", None, None),
    )
    return jax.shard_map(
        functools.partial(on_device, mesh.shape["pb"]),
        mesh=mesh,
        in_specs=placed,
        out_specs=P(("grp", "pb", "layer"), None),
        check_vma=False,
    )
```

```python
import functools

import jax
import jax.numpy as jnp
from jax import lax
from jax.experimental import pallas as pl
from jax.experimental.pallas import tpu as pltpu
from jax.sharding import PartitionSpec as P

F32, BF16 = jnp.float32, jnp.bfloat16
VMEM = pl.BlockSpec(memory_space=pltpu.VMEM)
HBM = pl.BlockSpec(memory_space=pl.ANY)
NT = (((1,), (1,)), ((), ()))
PARAMS = pltpu.CompilerParams(vmem_limit_bytes=24 * 1024 * 1024)


def estimate(flops, bytes_accessed):
    return pl.CostEstimate(flops=flops, bytes_accessed=bytes_accessed, transcendentals=0)


def selector_kernel(kin, chosen_ref):
    kout, grad = chosen_ref.shape[0] - kin, chosen_ref.shape[1]
    lane = lax.broadcasted_iota(jnp.int32, (kout, grad), 1)
    chosen_ref[:kout, :] = (lax.broadcasted_iota(jnp.int32, (kout, grad), 0) == lane // kin).astype(F32).astype(BF16)
    lane = lax.broadcasted_iota(jnp.int32, (kin, grad), 1)
    chosen_ref[kout:, :] = (lax.broadcasted_iota(jnp.int32, (kin, grad), 0) == lane % kin).astype(F32).astype(BF16)


def selectors(kout, kin):
    return pl.pallas_call(
        functools.partial(selector_kernel, kin),
        out_shape=jax.ShapeDtypeStruct((kout + kin, kout * kin), BF16),
        out_specs=VMEM,
        compiler_params=PARAMS,
        cost_estimate=estimate(2 * (kout * kin)**3, 0),
        name="selectors",
    )()


def select(matrices, chosen):
    rest, parts = jnp.concatenate(matrices, axis=0), []
    for _ in range(3):
        parts.append(rest.astype(BF16))
        rest = rest - parts[-1].astype(F32)
    product = jnp.dot(jnp.concatenate(parts, axis=0), chosen, preferred_element_type=F32)
    rows = rest.shape[0]
    return product[:rows] + product[rows:2 * rows] + product[2 * rows:]


def kron_kernel(basis_in, basis_out, eigen, chosen_ref, _, kron_ref, turned_ref, inverse_ref):
    kout, kin = basis_out.shape[1], basis_in.shape[1]
    repeat, tile = chosen_ref[:kout, :], chosen_ref[kout:, :]
    tiled = select([basis_in[0], basis_in[0].T, eigen[0]], tile)
    spread = select([basis_out[0], basis_out[0].T], repeat)
    tiled_in, turned_in, tiled_eigen = tiled[:kin], tiled[kin:2 * kin], tiled[2 * kin:]
    inverse_ref[...] = 1.0 / (jnp.sum(tiled_eigen * repeat.astype(F32), axis=0, keepdims=True) + 0.1)
    for b in range(kout):
        kron_ref[pl.ds(b * kin, kin), :] = (spread[b:b + 1, :] * tiled_in).astype(BF16)
    for a in range(kout):
        turned_ref[pl.ds(a * kin, kin), :] = (spread[kout + a:kout + a + 1, :] * turned_in).astype(BF16)


def kron_bases(basis_in, basis_out, eigenvalues, chosen, queries):
    grad = chosen.shape[1]
    return pl.pallas_call(
        kron_kernel,
        out_shape=tuple(jax.ShapeDtypeStruct(*x) for x in (((grad, grad), BF16), ((grad, grad), BF16), ((1, grad), F32))),
        in_specs=[VMEM] * 5,
        out_specs=(VMEM,) * 3,
        compiler_params=PARAMS,
        cost_estimate=estimate(grad**3 // 2, 0),
        name="kron_bases",
    )(basis_in, basis_out, eigenvalues, chosen, queries)


def precondition_kernel(*refs):
    *blocks, kron_ref, turned_ref, inverse_ref, w_ref = refs
    size, total = blocks[0].shape[0], w_ref.shape[0]
    for i, block in enumerate(blocks):
        w_ref[pl.ds(i * size, size), :] = block[...]
    step = min(total, 256)
    for i in range(total // step):
        rows = pl.ds(i * step, step)
        rotated = jnp.dot(w_ref[rows, :], kron_ref[...], preferred_element_type=F32)
        scaled = (rotated * inverse_ref[...]).astype(BF16)
        w_ref[rows, :] = jnp.dot(scaled, turned_ref[...], preferred_element_type=F32).astype(BF16)


def precondition(blocks, bases, name):
    rows, grad = sum(block.shape[0] for block in blocks), bases[0].shape[0]
    return pl.pallas_call(
        precondition_kernel,
        out_shape=jax.ShapeDtypeStruct((rows, grad), BF16),
        in_specs=[VMEM] * (len(blocks) + 3),
        out_specs=VMEM,
        compiler_params=PARAMS,
        cost_estimate=estimate((0 if name == "early_rows" else int(19.5 * grad**3)), 0),
        name=name,
    )(*blocks, *bases)


def arrange(masks, groups, w_ref):
    me, size = lax.axis_index("pb"), w_ref.shape[0] // len(masks)
    i = 0
    for group in groups:
        for row in range(0, group.shape[0], size):
            at = pl.multiple_of((me ^ masks[i]) * size, size) if len(masks) > 1 else 0
            w_ref[pl.ds(at, size), :] = group[pl.ds(row, size), :]
            i += 1


def first_kernel(masks, *refs):
    *groups, q_ref, out_ref, w_ref = refs
    arrange(masks, groups, w_ref)
    half, step = out_ref.shape[0], min(w_ref.shape[0], 256)
    own = pl.ds(pl.multiple_of(lax.axis_index("layer") * half, half), half)
    for i in range(w_ref.shape[0] // step):
        cols = slice(i * step, (i + 1) * step)
        out_ref[:, cols] = lax.dot_general(q_ref[own, :], w_ref[cols, :], NT, preferred_element_type=F32)


def last_kernel(masks, *refs):
    *groups, q_ref, first_ref, out_hbm, w_ref, out_ref, sems = refs
    arrange(masks, groups, w_ref)
    half, train, parts = first_ref.shape[0], w_ref.shape[0], sems.shape[0]
    step, rows = min(train, 256), half // parts
    copies = []
    for i in range(train // step):
        cols = slice(i * step, (i + 1) * step)
        second = lax.dot_general(q_ref[...], w_ref[cols, :], NT, preferred_element_type=F32)
        for r in range(parts):
            here = slice(r * rows, (r + 1) * rows)
            out_ref[here, cols] = (first_ref[here, cols] + second[here]).astype(BF16)
            if (i + 1) * step == train:
                copies.append(pltpu.make_async_copy(out_ref.at[here], out_hbm.at[here], sems.at[r]))
                copies[-1].start()
    for copy in copies:
        copy.wait()


def first_scores(masks, groups, queries):
    train, grad = sum(group.shape[0] for group in groups), queries.shape[1]
    half = queries.shape[0] // 2
    return pl.pallas_call(
        functools.partial(first_kernel, masks),
        out_shape=jax.ShapeDtypeStruct((half, train), F32),
        in_specs=[VMEM] * (len(groups) + 1),
        out_specs=VMEM,
        scratch_shapes=[pltpu.VMEM((train, grad), BF16)],
        compiler_params=PARAMS,
        cost_estimate=estimate(2 * train * grad * half, 2 * half * grad),
        name="first_scores",
    )(*groups, queries)


def last_scores(masks, groups, queries, first):
    train, grad = sum(group.shape[0] for group in groups), queries.shape[1]
    half = queries.shape[0]
    return pl.pallas_call(
        functools.partial(last_kernel, masks),
        out_shape=jax.ShapeDtypeStruct((half, train), BF16),
        in_specs=[VMEM] * (len(groups) + 2),
        out_specs=HBM,
        scratch_shapes=[pltpu.VMEM((train, grad), BF16), pltpu.VMEM((half, train), BF16), pltpu.SemaphoreType.DMA((8,))],
        compiler_params=PARAMS,
        cost_estimate=estimate(2 * train * grad * half, 2 * half * grad),
        name="last_scores",
    )(*groups, queries, first)


def theirs_kernel(q_ref, theirs_ref):
    half = theirs_ref.shape[0]
    start, rows = (1 - lax.axis_index("layer")) * half, min(half, 256)
    for i in range(half // rows):
        there = pl.ds(pl.multiple_of(start + i * rows, rows), rows)
        theirs_ref[pl.ds(i * rows, rows), :] = q_ref[there, :]


def other_half(queries):
    rows, grad = queries.shape
    return pl.pallas_call(
        theirs_kernel,
        out_shape=jax.ShapeDtypeStruct((rows // 2, grad), BF16),
        in_specs=[VMEM],
        out_specs=VMEM,
        compiler_params=PARAMS,
        cost_estimate=estimate(4 * grad**3, 0),
        name="other_half",
    )(queries)


def exchange(x, n, mask):
    return lax.ppermute(x, "pb", [(i, i ^ mask) for i in range(n)])


def other_layer(x):
    return lax.ppermute(x, "layer", [(0, 1), (1, 0)])


def on_device(n, query_grads, train_grads, basis_in, basis_out, eigenvalues):
    train = train_grads.reshape(train_grads.shape[0], -1)
    queries = query_grads.reshape(query_grads.shape[0], -1)
    chosen = selectors(basis_out.shape[1], basis_in.shape[1])
    if n == 8:
        far = [exchange(train, n, mask) for mask in (4, 6)]
        behind, chosen = lax.optimization_barrier((train, chosen))
        near = [exchange(behind, n, mask) for mask in (2, 1, 3)]
        groups, masks = [[train] + far + near, [exchange(block, n, 1) for block in far]], (0, 4, 6, 2, 1, 3, 5, 7)
        loose, = lax.optimization_barrier((queries,))
        sent, _ = lax.optimization_barrier((other_half(loose), near[1]))
    else:
        groups, masks = [[lax.all_gather(train, "pb", axis=0, tiled=True)]], (0,)
        sent = other_half(queries)
    other_queries = other_layer(sent)
    bases = kron_bases(basis_in, basis_out, eigenvalues, chosen, queries)
    own = [precondition(groups[0], bases, "early_rows")]
    if len(groups) > 1:
        own.append(precondition(groups[1], bases, "late_rows"))
    other = [other_layer(w) for w in own]
    return last_scores(masks, other, other_queries, first_scores(masks, own, queries))


def solution(mesh):
    placed = (
        P(("grp", "pb"), "layer", None),
        P(("grp", "pb"), "layer", None),
        P("layer", None, None),
        P("layer", None, None),
        P("layer", None, None),
    )
    return jax.shard_map(
        functools.partial(on_device, mesh.shape["pb"]),
        mesh=mesh,
        in_specs=placed,
        out_specs=P(("grp", "pb", "layer"), None),
        check_vma=False,
    )
```

```python
import functools

import jax
import jax.numpy as jnp
from jax import lax
from jax.experimental import pallas as pl
from jax.experimental.pallas import tpu as pltpu
from jax.sharding import PartitionSpec as P

F32, BF16 = jnp.float32, jnp.bfloat16
VMEM = pl.BlockSpec(memory_space=pltpu.VMEM)
HBM = pl.BlockSpec(memory_space=pl.ANY)
NT = (((1,), (1,)), ((), ()))
PARAMS = pltpu.CompilerParams(vmem_limit_bytes=24 * 1024 * 1024)


def estimate(flops, bytes_accessed):
    return pl.CostEstimate(flops=flops, bytes_accessed=bytes_accessed, transcendentals=0)


def selector_kernel(kin, chosen_ref):
    kout, grad = chosen_ref.shape[0] - kin, chosen_ref.shape[1]
    lane = lax.broadcasted_iota(jnp.int32, (kout, grad), 1)
    chosen_ref[:kout, :] = (lax.broadcasted_iota(jnp.int32, (kout, grad), 0) == lane // kin).astype(F32).astype(BF16)
    lane = lax.broadcasted_iota(jnp.int32, (kin, grad), 1)
    chosen_ref[kout:, :] = (lax.broadcasted_iota(jnp.int32, (kin, grad), 0) == lane % kin).astype(F32).astype(BF16)


def selectors(kout, kin):
    return pl.pallas_call(
        functools.partial(selector_kernel, kin),
        out_shape=jax.ShapeDtypeStruct((kout + kin, kout * kin), BF16),
        out_specs=VMEM,
        compiler_params=PARAMS,
        cost_estimate=estimate(2 * (kout * kin)**3, 0),
        name="selectors",
    )()


def select(matrices, chosen):
    rest, parts = jnp.concatenate(matrices, axis=0), []
    for _ in range(3):
        parts.append(rest.astype(BF16))
        rest = rest - parts[-1].astype(F32)
    product = jnp.dot(jnp.concatenate(parts, axis=0), chosen, preferred_element_type=F32)
    rows = rest.shape[0]
    return product[:rows] + product[rows:2 * rows] + product[2 * rows:]


def kron_kernel(basis_in, basis_out, eigen, chosen_ref, _, kron_ref, turned_ref, inverse_ref):
    kout, kin = basis_out.shape[1], basis_in.shape[1]
    repeat, tile = chosen_ref[:kout, :], chosen_ref[kout:, :]
    tiled = select([basis_in[0], basis_in[0].T, eigen[0]], tile)
    spread = select([basis_out[0], basis_out[0].T], repeat)
    tiled_in, turned_in, tiled_eigen = tiled[:kin], tiled[kin:2 * kin], tiled[2 * kin:]
    inverse_ref[...] = 1.0 / (jnp.sum(tiled_eigen * repeat.astype(F32), axis=0, keepdims=True) + 0.1)
    for b in range(kout):
        kron_ref[pl.ds(b * kin, kin), :] = (spread[b:b + 1, :] * tiled_in).astype(BF16)
    for a in range(kout):
        turned_ref[pl.ds(a * kin, kin), :] = (spread[kout + a:kout + a + 1, :] * turned_in).astype(BF16)


def kron_bases(basis_in, basis_out, eigenvalues, chosen, queries):
    grad = chosen.shape[1]
    return pl.pallas_call(
        kron_kernel,
        out_shape=tuple(jax.ShapeDtypeStruct(*x) for x in (((grad, grad), BF16), ((grad, grad), BF16), ((1, grad), F32))),
        in_specs=[VMEM] * 5,
        out_specs=(VMEM,) * 3,
        compiler_params=PARAMS,
        cost_estimate=estimate(grad**3 // 2, 0),
        name="kron_bases",
    )(basis_in, basis_out, eigenvalues, chosen, queries)


def precondition_kernel(*refs):
    *blocks, kron_ref, turned_ref, inverse_ref, w_ref = refs
    row, total = 0, w_ref.shape[0]
    for block in blocks:
        w_ref[pl.ds(row, block.shape[0]), :] = block[...]
        row += block.shape[0]
    step = min(total, 256)
    for i in range(total // step):
        rows = pl.ds(i * step, step)
        rotated = jnp.dot(w_ref[rows, :], kron_ref[...], preferred_element_type=F32)
        scaled = (rotated * inverse_ref[...]).astype(BF16)
        w_ref[rows, :] = jnp.dot(scaled, turned_ref[...], preferred_element_type=F32).astype(BF16)


def precondition(blocks, bases, name):
    rows, grad = sum(block.shape[0] for block in blocks), bases[0].shape[0]
    return pl.pallas_call(
        precondition_kernel,
        out_shape=jax.ShapeDtypeStruct((rows, grad), BF16),
        in_specs=[VMEM] * (len(blocks) + 3),
        out_specs=VMEM,
        compiler_params=PARAMS,
        cost_estimate=estimate((0 if name == "early_rows" else int(18.5 * grad**3)), 0),
        name=name,
    )(*blocks, *bases)


def arrange(masks, groups, w_ref):
    me, size = lax.axis_index("pb"), w_ref.shape[0] // len(masks)
    i = 0
    for group in groups:
        for row in range(0, group.shape[0], size):
            at = pl.multiple_of((me ^ masks[i]) * size, size) if len(masks) > 1 else 0
            w_ref[pl.ds(at, size), :] = group[pl.ds(row, size), :]
            i += 1


def first_kernel(masks, *refs):
    *groups, q_ref, out_ref, w_ref = refs
    arrange(masks, groups, w_ref)
    half, step = out_ref.shape[0], min(w_ref.shape[0], 256)
    own = pl.ds(pl.multiple_of(lax.axis_index("layer") * half, half), half)
    for i in range(w_ref.shape[0] // step):
        cols = slice(i * step, (i + 1) * step)
        out_ref[:, cols] = lax.dot_general(q_ref[own, :], w_ref[cols, :], NT, preferred_element_type=F32)


def last_kernel(masks, *refs):
    *groups, q_ref, first_ref, out_hbm, w_ref, out_ref, sems = refs
    arrange(masks, groups, w_ref)
    half, train, parts = first_ref.shape[0], w_ref.shape[0], sems.shape[0]
    step, rows = min(train, 256), half // parts
    copies = []
    for i in range(train // step):
        cols = slice(i * step, (i + 1) * step)
        second = lax.dot_general(q_ref[...], w_ref[cols, :], NT, preferred_element_type=F32)
        for r in range(parts):
            here = slice(r * rows, (r + 1) * rows)
            out_ref[here, cols] = (first_ref[here, cols] + second[here]).astype(BF16)
            if (i + 1) * step == train:
                copies.append(pltpu.make_async_copy(out_ref.at[here], out_hbm.at[here], sems.at[r]))
                copies[-1].start()
    for copy in copies:
        copy.wait()


def first_scores(masks, groups, queries):
    train, grad = sum(group.shape[0] for group in groups), queries.shape[1]
    half = queries.shape[0] // 2
    return pl.pallas_call(
        functools.partial(first_kernel, masks),
        out_shape=jax.ShapeDtypeStruct((half, train), F32),
        in_specs=[VMEM] * (len(groups) + 1),
        out_specs=VMEM,
        scratch_shapes=[pltpu.VMEM((train, grad), BF16)],
        compiler_params=PARAMS,
        cost_estimate=estimate(2 * train * grad * half, 2 * half * grad),
        name="first_scores",
    )(*groups, queries)


def last_scores(masks, groups, queries, first):
    train, grad = sum(group.shape[0] for group in groups), queries.shape[1]
    half = queries.shape[0]
    return pl.pallas_call(
        functools.partial(last_kernel, masks),
        out_shape=jax.ShapeDtypeStruct((half, train), BF16),
        in_specs=[VMEM] * (len(groups) + 2),
        out_specs=HBM,
        scratch_shapes=[pltpu.VMEM((train, grad), BF16), pltpu.VMEM((half, train), BF16), pltpu.SemaphoreType.DMA((8,))],
        compiler_params=PARAMS,
        cost_estimate=estimate(2 * train * grad * half, 2 * half * grad),
        name="last_scores",
    )(*groups, queries, first)


def theirs_kernel(q_ref, theirs_ref):
    half = theirs_ref.shape[0]
    start, rows = (1 - lax.axis_index("layer")) * half, min(half, 256)
    for i in range(half // rows):
        there = pl.ds(pl.multiple_of(start + i * rows, rows), rows)
        theirs_ref[pl.ds(i * rows, rows), :] = q_ref[there, :]


def other_half(queries):
    rows, grad = queries.shape
    return pl.pallas_call(
        theirs_kernel,
        out_shape=jax.ShapeDtypeStruct((rows // 2, grad), BF16),
        in_specs=[VMEM],
        out_specs=VMEM,
        compiler_params=PARAMS,
        cost_estimate=estimate(4 * grad**3, 0),
        name="other_half",
    )(queries)


def join_kernel(first_ref, second_ref, out_ref):
    rows = first_ref.shape[0]
    out_ref[:rows, :] = first_ref[...]
    out_ref[rows:, :] = second_ref[...]


def join(first, second):
    return pl.pallas_call(
        join_kernel,
        out_shape=jax.ShapeDtypeStruct((2 * first.shape[0], first.shape[1]), BF16),
        in_specs=[VMEM] * 2,
        out_specs=VMEM,
        compiler_params=PARAMS,
        cost_estimate=estimate(0, 0),
        name="join_blocks",
    )(first, second)


def exchange(x, n, mask):
    return lax.ppermute(x, "pb", [(i, i ^ mask) for i in range(n)])


def other_layer(x):
    return lax.ppermute(x, "layer", [(0, 1), (1, 0)])


def on_device(n, query_grads, train_grads, basis_in, basis_out, eigenvalues):
    train = train_grads.reshape(train_grads.shape[0], -1)
    queries = query_grads.reshape(query_grads.shape[0], -1)
    chosen = selectors(basis_out.shape[1], basis_in.shape[1])
    if n == 8:
        got = {mask: exchange(train, n, mask) for mask in (4,)}
        behind, chosen = lax.optimization_barrier((train, chosen))
        got.update({mask: exchange(behind, n, mask) for mask in (2, 1, 3)})
        late = [exchange(got[4], n, 3), exchange(got[4], n, 2), exchange(got[4], n, 1)]
        masks = (0, *got, 7, 6, 5)
        groups = [[train] + list(got.values()), late]
        loose, = lax.optimization_barrier((queries,))
        sent, _ = lax.optimization_barrier((other_half(loose), got[1]))
    else:
        groups, masks = [[lax.all_gather(train, "pb", axis=0, tiled=True)]], (0,)
        sent = other_half(queries)
    other_queries = other_layer(sent)
    bases = kron_bases(basis_in, basis_out, eigenvalues, chosen, queries)
    own = [precondition(groups[0], bases, "early_rows")]
    if len(groups) > 1:
        own.append(precondition(groups[1], bases, "late_rows"))
    other = [other_layer(w) for w in own]
    return last_scores(masks, other, other_queries, first_scores(masks, own, queries))


def solution(mesh):
    placed = (
        P(("grp", "pb"), "layer", None),
        P(("grp", "pb"), "layer", None),
        P("layer", None, None),
        P("layer", None, None),
        P("layer", None, None),
    )
    return jax.shard_map(
        functools.partial(on_device, mesh.shape["pb"]),
        mesh=mesh,
        in_specs=placed,
        out_specs=P(("grp", "pb", "layer"), None),
        check_vma=False,
    )
```

```python
import functools

import jax
import jax.numpy as jnp
from jax import lax
from jax.experimental import pallas as pl
from jax.experimental.pallas import tpu as pltpu
from jax.sharding import PartitionSpec as P

F32, BF16 = jnp.float32, jnp.bfloat16
VMEM = pl.BlockSpec(memory_space=pltpu.VMEM)
HBM = pl.BlockSpec(memory_space=pl.ANY)
NT = (((1,), (1,)), ((), ()))
PARAMS = pltpu.CompilerParams(vmem_limit_bytes=24 * 1024 * 1024)


def estimate(flops, bytes_accessed):
    return pl.CostEstimate(flops=flops, bytes_accessed=bytes_accessed, transcendentals=0)


def selector_kernel(kin, chosen_ref):
    kout, grad = chosen_ref.shape[0] - kin, chosen_ref.shape[1]
    lane = lax.broadcasted_iota(jnp.int32, (kout, grad), 1)
    chosen_ref[:kout, :] = (lax.broadcasted_iota(jnp.int32, (kout, grad), 0) == lane // kin).astype(F32).astype(BF16)
    lane = lax.broadcasted_iota(jnp.int32, (kin, grad), 1)
    chosen_ref[kout:, :] = (lax.broadcasted_iota(jnp.int32, (kin, grad), 0) == lane % kin).astype(F32).astype(BF16)


def selectors(kout, kin):
    return pl.pallas_call(
        functools.partial(selector_kernel, kin),
        out_shape=jax.ShapeDtypeStruct((kout + kin, kout * kin), BF16),
        out_specs=VMEM,
        compiler_params=PARAMS,
        cost_estimate=estimate(2 * (kout * kin)**3, 0),
        name="selectors",
    )()


def select(matrices, chosen):
    rest, parts = jnp.concatenate(matrices, axis=0), []
    for _ in range(3):
        parts.append(rest.astype(BF16))
        rest = rest - parts[-1].astype(F32)
    product = jnp.dot(jnp.concatenate(parts, axis=0), chosen, preferred_element_type=F32)
    rows = rest.shape[0]
    return product[:rows] + product[rows:2 * rows] + product[2 * rows:]


def kron_kernel(basis_in, basis_out, eigen, chosen_ref, _, kron_ref, turned_ref, inverse_ref):
    kout, kin = basis_out.shape[1], basis_in.shape[1]
    repeat, tile = chosen_ref[:kout, :], chosen_ref[kout:, :]
    tiled = select([basis_in[0], basis_in[0].T, eigen[0]], tile)
    spread = select([basis_out[0], basis_out[0].T], repeat)
    tiled_in, turned_in, tiled_eigen = tiled[:kin], tiled[kin:2 * kin], tiled[2 * kin:]
    inverse_ref[...] = 1.0 / (jnp.sum(tiled_eigen * repeat.astype(F32), axis=0, keepdims=True) + 0.1)
    for b in range(kout):
        kron_ref[pl.ds(b * kin, kin), :] = (spread[b:b + 1, :] * tiled_in).astype(BF16)
    for a in range(kout):
        turned_ref[pl.ds(a * kin, kin), :] = (spread[kout + a:kout + a + 1, :] * turned_in).astype(BF16)


def kron_bases(basis_in, basis_out, eigenvalues, chosen, queries):
    grad = chosen.shape[1]
    return pl.pallas_call(
        kron_kernel,
        out_shape=tuple(jax.ShapeDtypeStruct(*x) for x in (((grad, grad), BF16), ((grad, grad), BF16), ((1, grad), F32))),
        in_specs=[VMEM] * 5,
        out_specs=(VMEM,) * 3,
        compiler_params=PARAMS,
        cost_estimate=estimate(grad**3 // 2, 0),
        name="kron_bases",
    )(basis_in, basis_out, eigenvalues, chosen, queries)


def precondition_kernel(*refs):
    *blocks, kron_ref, turned_ref, inverse_ref, w_ref = refs
    size, total = blocks[0].shape[0], w_ref.shape[0]
    for i, block in enumerate(blocks):
        w_ref[pl.ds(i * size, size), :] = block[...]
    step = min(total, 256)
    for i in range(total // step):
        rows = pl.ds(i * step, step)
        rotated = jnp.dot(w_ref[rows, :], kron_ref[...], preferred_element_type=F32)
        scaled = (rotated * inverse_ref[...]).astype(BF16)
        w_ref[rows, :] = jnp.dot(scaled, turned_ref[...], preferred_element_type=F32).astype(BF16)


def precondition(blocks, bases, name):
    rows, grad = sum(block.shape[0] for block in blocks), bases[0].shape[0]
    return pl.pallas_call(
        precondition_kernel,
        out_shape=jax.ShapeDtypeStruct((rows, grad), BF16),
        in_specs=[VMEM] * (len(blocks) + 3),
        out_specs=VMEM,
        compiler_params=PARAMS,
        cost_estimate=estimate((0 if name == "early_rows" else int(19.5 * grad**3)), 0),
        name=name,
    )(*blocks, *bases)


def arrange(masks, groups, w_ref):
    me, size = lax.axis_index("pb"), w_ref.shape[0] // len(masks)
    i = 0
    for group in groups:
        for row in range(0, group.shape[0], size):
            at = pl.multiple_of((me ^ masks[i]) * size, size) if len(masks) > 1 else 0
            w_ref[pl.ds(at, size), :] = group[pl.ds(row, size), :]
            i += 1


def first_kernel(masks, *refs):
    *groups, q_ref, out_ref, w_ref = refs
    arrange(masks, groups, w_ref)
    half, step = out_ref.shape[0], min(w_ref.shape[0], 256)
    own = pl.ds(pl.multiple_of(lax.axis_index("layer") * half, half), half)
    for i in range(w_ref.shape[0] // step):
        cols = slice(i * step, (i + 1) * step)
        out_ref[:, cols] = lax.dot_general(q_ref[own, :], w_ref[cols, :], NT, preferred_element_type=F32)


def last_kernel(masks, *refs):
    *groups, q_ref, first_ref, out_hbm, w_ref, out_ref, sems = refs
    arrange(masks, groups, w_ref)
    half, train, parts = first_ref.shape[0], w_ref.shape[0], sems.shape[0]
    step, rows = min(train, 256), half // parts
    copies = []
    for i in range(train // step):
        cols = slice(i * step, (i + 1) * step)
        second = lax.dot_general(q_ref[...], w_ref[cols, :], NT, preferred_element_type=F32)
        for r in range(parts):
            here = slice(r * rows, (r + 1) * rows)
            out_ref[here, cols] = (first_ref[here, cols] + second[here]).astype(BF16)
            if (i + 1) * step == train:
                copies.append(pltpu.make_async_copy(out_ref.at[here], out_hbm.at[here], sems.at[r]))
                copies[-1].start(priority=r % 2)
    for copy in copies:
        copy.wait()


def first_scores(masks, groups, queries):
    train, grad = sum(group.shape[0] for group in groups), queries.shape[1]
    half = queries.shape[0] // 2
    return pl.pallas_call(
        functools.partial(first_kernel, masks),
        out_shape=jax.ShapeDtypeStruct((half, train), F32),
        in_specs=[VMEM] * (len(groups) + 1),
        out_specs=VMEM,
        scratch_shapes=[pltpu.VMEM((train, grad), BF16)],
        compiler_params=PARAMS,
        cost_estimate=estimate(2 * train * grad * half, 2 * half * grad),
        name="first_scores",
    )(*groups, queries)


def last_scores(masks, groups, queries, first):
    train, grad = sum(group.shape[0] for group in groups), queries.shape[1]
    half = queries.shape[0]
    return pl.pallas_call(
        functools.partial(last_kernel, masks),
        out_shape=jax.ShapeDtypeStruct((half, train), BF16),
        in_specs=[VMEM] * (len(groups) + 2),
        out_specs=HBM,
        scratch_shapes=[pltpu.VMEM((train, grad), BF16), pltpu.VMEM((half, train), BF16), pltpu.SemaphoreType.DMA((8,))],
        compiler_params=PARAMS,
        cost_estimate=estimate(2 * train * grad * half, 2 * half * grad),
        name="last_scores",
    )(*groups, queries, first)


def theirs_kernel(q_ref, theirs_ref):
    half = theirs_ref.shape[0]
    start, rows = (1 - lax.axis_index("layer")) * half, min(half, 256)
    for i in range(half // rows):
        there = pl.ds(pl.multiple_of(start + i * rows, rows), rows)
        theirs_ref[pl.ds(i * rows, rows), :] = q_ref[there, :]


def other_half(queries):
    rows, grad = queries.shape
    return pl.pallas_call(
        theirs_kernel,
        out_shape=jax.ShapeDtypeStruct((rows // 2, grad), BF16),
        in_specs=[VMEM],
        out_specs=VMEM,
        compiler_params=PARAMS,
        cost_estimate=estimate(4 * grad**3, 0),
        name="other_half",
    )(queries)


def exchange(x, n, mask):
    return lax.ppermute(x, "pb", [(i, i ^ mask) for i in range(n)])


def other_layer(x):
    return lax.ppermute(x, "layer", [(0, 1), (1, 0)])


def on_device(n, query_grads, train_grads, basis_in, basis_out, eigenvalues):
    train = train_grads.reshape(train_grads.shape[0], -1)
    queries = query_grads.reshape(query_grads.shape[0], -1)
    chosen = selectors(basis_out.shape[1], basis_in.shape[1])
    if n == 8:
        far = [exchange(train, n, mask) for mask in (4, 6)]
        behind, chosen = lax.optimization_barrier((train, chosen))
        near = [exchange(behind, n, mask) for mask in (2, 1, 3)]
        groups, masks = [[train] + far + near, [exchange(block, n, 1) for block in far]], (0, 4, 6, 2, 1, 3, 5, 7)
        loose, = lax.optimization_barrier((queries,))
        sent, _ = lax.optimization_barrier((other_half(loose), near[1]))
    else:
        groups, masks = [[lax.all_gather(train, "pb", axis=0, tiled=True)]], (0,)
        sent = other_half(queries)
    other_queries = other_layer(sent)
    bases = kron_bases(basis_in, basis_out, eigenvalues, chosen, queries)
    own = [precondition(groups[0], bases, "early_rows")]
    if len(groups) > 1:
        own.append(precondition(groups[1], bases, "late_rows"))
    other = [other_layer(w) for w in own]
    return last_scores(masks, other, other_queries, first_scores(masks, own, queries))


def solution(mesh):
    placed = (
        P(("grp", "pb"), "layer", None),
        P(("grp", "pb"), "layer", None),
        P("layer", None, None),
        P("layer", None, None),
        P("layer", None, None),
    )
    return jax.shard_map(
        functools.partial(on_device, mesh.shape["pb"]),
        mesh=mesh,
        in_specs=placed,
        out_specs=P(("grp", "pb", "layer"), None),
        check_vma=False,
    )
```

```python
import functools

import jax
import jax.numpy as jnp
from jax import lax
from jax.experimental import pallas as pl
from jax.experimental.pallas import tpu as pltpu
from jax.sharding import PartitionSpec as P

F32, BF16 = jnp.float32, jnp.bfloat16
VMEM = pl.BlockSpec(memory_space=pltpu.VMEM)
HBM = pl.BlockSpec(memory_space=pl.ANY)
NT = (((1,), (1,)), ((), ()))
PARAMS = pltpu.CompilerParams(vmem_limit_bytes=24 * 1024 * 1024)


def estimate(flops, bytes_accessed):
    return pl.CostEstimate(flops=flops, bytes_accessed=bytes_accessed, transcendentals=0)


def selector_kernel(kin, chosen_ref):
    kout, grad = chosen_ref.shape[0] - kin, chosen_ref.shape[1]
    lane = lax.broadcasted_iota(jnp.int32, (kout, grad), 1)
    chosen_ref[:kout, :] = (lax.broadcasted_iota(jnp.int32, (kout, grad), 0) == lane // kin).astype(F32).astype(BF16)
    lane = lax.broadcasted_iota(jnp.int32, (kin, grad), 1)
    chosen_ref[kout:, :] = (lax.broadcasted_iota(jnp.int32, (kin, grad), 0) == lane % kin).astype(F32).astype(BF16)


def selectors(kout, kin):
    return pl.pallas_call(
        functools.partial(selector_kernel, kin),
        out_shape=jax.ShapeDtypeStruct((kout + kin, kout * kin), BF16),
        out_specs=VMEM,
        compiler_params=PARAMS,
        cost_estimate=estimate(2 * (kout * kin)**3, 0),
        name="selectors",
    )()


def select(matrices, chosen):
    rest, parts = jnp.concatenate(matrices, axis=0), []
    for _ in range(3):
        parts.append(rest.astype(BF16))
        rest = rest - parts[-1].astype(F32)
    product = jnp.dot(jnp.concatenate(parts, axis=0), chosen, preferred_element_type=F32)
    rows = rest.shape[0]
    return product[:rows] + product[rows:2 * rows] + product[2 * rows:]


def kron_kernel(basis_in, basis_out, eigen, chosen_ref, _, kron_ref, turned_ref, inverse_ref):
    kout, kin = basis_out.shape[1], basis_in.shape[1]
    repeat, tile = chosen_ref[:kout, :], chosen_ref[kout:, :]
    tiled = select([basis_in[0], basis_in[0].T, eigen[0]], tile)
    spread = select([basis_out[0], basis_out[0].T], repeat)
    tiled_in, turned_in, tiled_eigen = tiled[:kin], tiled[kin:2 * kin], tiled[2 * kin:]
    inverse_ref[...] = 1.0 / (jnp.sum(tiled_eigen * repeat.astype(F32), axis=0, keepdims=True) + 0.1)
    for b in range(kout):
        kron_ref[pl.ds(b * kin, kin), :] = (spread[b:b + 1, :] * tiled_in).astype(BF16)
    for a in range(kout):
        turned_ref[pl.ds(a * kin, kin), :] = (spread[kout + a:kout + a + 1, :] * turned_in).astype(BF16)


def kron_bases(basis_in, basis_out, eigenvalues, chosen, queries):
    grad = chosen.shape[1]
    return pl.pallas_call(
        kron_kernel,
        out_shape=tuple(jax.ShapeDtypeStruct(*x) for x in (((grad, grad), BF16), ((grad, grad), BF16), ((1, grad), F32))),
        in_specs=[VMEM] * 5,
        out_specs=(VMEM,) * 3,
        compiler_params=PARAMS,
        cost_estimate=estimate(grad**3 // 2, 0),
        name="kron_bases",
    )(basis_in, basis_out, eigenvalues, chosen, queries)


def precondition_kernel(*refs):
    *blocks, kron_ref, turned_ref, inverse_ref, w_ref = refs
    size, total = blocks[0].shape[0], w_ref.shape[0]
    for i, block in enumerate(blocks):
        w_ref[pl.ds(i * size, size), :] = block[...]
    step = min(total, 256)
    for i in range(total // step):
        rows = pl.ds(i * step, step)
        rotated = jnp.dot(w_ref[rows, :], kron_ref[...], preferred_element_type=F32)
        scaled = (rotated * inverse_ref[...]).astype(BF16)
        w_ref[rows, :] = jnp.dot(scaled, turned_ref[...], preferred_element_type=F32).astype(BF16)


def precondition(blocks, bases, name):
    rows, grad = sum(block.shape[0] for block in blocks), bases[0].shape[0]
    return pl.pallas_call(
        precondition_kernel,
        out_shape=jax.ShapeDtypeStruct((rows, grad), BF16),
        in_specs=[VMEM] * (len(blocks) + 3),
        out_specs=VMEM,
        compiler_params=PARAMS,
        cost_estimate=estimate((0 if name == "early_rows" else int(19.5 * grad**3)), 0),
        name=name,
    )(*blocks, *bases)


def arrange(masks, groups, w_ref):
    me, size = lax.axis_index("pb"), w_ref.shape[0] // len(masks)
    i = 0
    for group in groups:
        for row in range(0, group.shape[0], size):
            at = pl.multiple_of((me ^ masks[i]) * size, size) if len(masks) > 1 else 0
            w_ref[pl.ds(at, size), :] = group[pl.ds(row, size), :]
            i += 1


def first_kernel(masks, *refs):
    *groups, q_ref, out_ref, w_ref = refs
    arrange(masks, groups, w_ref)
    half, step = out_ref.shape[0], min(w_ref.shape[0], 256)
    own = pl.ds(pl.multiple_of(lax.axis_index("layer") * half, half), half)
    for i in range(w_ref.shape[0] // step):
        cols = slice(i * step, (i + 1) * step)
        out_ref[:, cols] = lax.dot_general(q_ref[own, :], w_ref[cols, :], NT, preferred_element_type=F32)


def last_kernel(masks, *refs):
    *groups, q_ref, first_ref, out_hbm, w_ref, out_ref, sems = refs
    arrange(masks, groups, w_ref)
    half, train, parts = first_ref.shape[0], w_ref.shape[0], sems.shape[0]
    step, rows = min(train, 256), half // parts
    copies = []
    for i in range(train // step):
        cols = slice(i * step, (i + 1) * step)
        second = lax.dot_general(q_ref[...], w_ref[cols, :], NT, preferred_element_type=F32)
        for r in range(parts):
            here = slice(r * rows, (r + 1) * rows)
            out_ref[here, cols] = (first_ref[here, cols] + second[here]).astype(BF16)
            if (i + 1) * step == train:
                copies.append(pltpu.make_async_copy(out_ref.at[here], out_hbm.at[here], sems.at[r]))
                copies[-1].start()
    for copy in copies:
        copy.wait()


def first_scores(masks, groups, queries):
    train, grad = sum(group.shape[0] for group in groups), queries.shape[1]
    half = queries.shape[0] // 2
    return pl.pallas_call(
        functools.partial(first_kernel, masks),
        out_shape=jax.ShapeDtypeStruct((half, train), F32),
        in_specs=[VMEM] * (len(groups) + 1),
        out_specs=VMEM,
        scratch_shapes=[pltpu.VMEM((train, grad), BF16)],
        compiler_params=PARAMS,
        cost_estimate=estimate(2 * train * grad * half, 2 * half * grad),
        name="first_scores",
    )(*groups, queries)


def last_scores(masks, groups, queries, first):
    train, grad = sum(group.shape[0] for group in groups), queries.shape[1]
    half = queries.shape[0]
    return pl.pallas_call(
        functools.partial(last_kernel, masks),
        out_shape=jax.ShapeDtypeStruct((half, train), BF16),
        in_specs=[VMEM] * (len(groups) + 2),
        out_specs=HBM,
        scratch_shapes=[pltpu.VMEM((train, grad), BF16), pltpu.VMEM((half, train), BF16), pltpu.SemaphoreType.DMA((16,))],
        compiler_params=PARAMS,
        cost_estimate=estimate(2 * train * grad * half, 2 * half * grad),
        name="last_scores",
    )(*groups, queries, first)


def theirs_kernel(q_ref, theirs_ref):
    half = theirs_ref.shape[0]
    start, rows = (1 - lax.axis_index("layer")) * half, min(half, 256)
    for i in range(half // rows):
        there = pl.ds(pl.multiple_of(start + i * rows, rows), rows)
        theirs_ref[pl.ds(i * rows, rows), :] = q_ref[there, :]


def other_half(queries):
    rows, grad = queries.shape
    return pl.pallas_call(
        theirs_kernel,
        out_shape=jax.ShapeDtypeStruct((rows // 2, grad), BF16),
        in_specs=[VMEM],
        out_specs=VMEM,
        compiler_params=PARAMS,
        cost_estimate=estimate(4 * grad**3, 0),
        name="other_half",
    )(queries)


def exchange(x, n, mask):
    return lax.ppermute(x, "pb", [(i, i ^ mask) for i in range(n)])


def other_layer(x):
    return lax.ppermute(x, "layer", [(0, 1), (1, 0)])


def on_device(n, query_grads, train_grads, basis_in, basis_out, eigenvalues):
    train = train_grads.reshape(train_grads.shape[0], -1)
    queries = query_grads.reshape(query_grads.shape[0], -1)
    chosen = selectors(basis_out.shape[1], basis_in.shape[1])
    if n == 8:
        far = [exchange(train, n, mask) for mask in (4, 6)]
        behind, chosen = lax.optimization_barrier((train, chosen))
        near = [exchange(behind, n, mask) for mask in (2, 1, 3)]
        groups, masks = [[train] + far + near, [exchange(block, n, 1) for block in far]], (0, 4, 6, 2, 1, 3, 5, 7)
        loose, = lax.optimization_barrier((queries,))
        sent, _ = lax.optimization_barrier((other_half(loose), near[1]))
    else:
        groups, masks = [[lax.all_gather(train, "pb", axis=0, tiled=True)]], (0,)
        sent = other_half(queries)
    other_queries = other_layer(sent)
    bases = kron_bases(basis_in, basis_out, eigenvalues, chosen, queries)
    own = [precondition(groups[0], bases, "early_rows")]
    if len(groups) > 1:
        own.append(precondition(groups[1], bases, "late_rows"))
    other = [other_layer(w) for w in own]
    return last_scores(masks, other, other_queries, first_scores(masks, own, queries))


def solution(mesh):
    placed = (
        P(("grp", "pb"), "layer", None),
        P(("grp", "pb"), "layer", None),
        P("layer", None, None),
        P("layer", None, None),
        P("layer", None, None),
    )
    return jax.shard_map(
        functools.partial(on_device, mesh.shape["pb"]),
        mesh=mesh,
        in_specs=placed,
        out_specs=P(("grp", "pb", "layer"), None),
        check_vma=False,
    )
```
